32 devices in a mesh: vocab: 8 (over z, x), width: 4 (over y, core).
Axes of the slice: x: 2, y: 2, z: 4, core: 2. Of those that a mesh axis runs over, the one named last changes fastest.
Arguments:
- hidden: bfloat16 [8192, 1024], P('vocab', 'width'), may hold values from -60 to 60
- norm_gain: float32 [1024], P('width'), may hold values from 0.5 to 1.5
- head_weight: bfloat16 [1024, 32128], P('width', 'vocab'), may hold values from -1 to 1
- token_ids: int32 [8192], P('width'), may hold values from 0 to 32127
- seq_lengths: int32 [4], replicated, may hold values from 1 to 2048, as said below
Outputs:
- log_probs: float32 [8192], P('width')
- entropies: float32 [8192], P('width')
The draws below stay inside these ranges and needn't reach their ends.
Inputs may be any that keep to these rules, and one draw needn't show every extreme that they name: `seq_lengths`: each sequence has 1 to 2048 live tokens at its start; some sequence has exactly 2048.
All inputs are finite; a program needn't handle non-finite values.
Results may differ from the reference program's by a relative error of at most 0.0041.
Values may be sent and summed in bfloat16 or wider, within the bound.
No kernel may reach another device: no remote copies, remote signals or barrier semaphores. Data moves between devices by JAX's collectives and lax.ppermute only.
A program may use at most 320 MiB of HBM per device.

```python
import math
import jax
import jax.numpy as jnp
from jax import lax

D = 1024
V = 32128
TOK_DEV = 1024
TOKENS = 8192
SEQ_LEN = 2048
SEQS = 4


def draw_hidden(key, part):
    key_main, key_rows, key_cols = jax.random.split(jax.random.fold_in(key, 1), 3)
    row_scale = jnp.exp(jax.random.uniform(key_rows, (TOKENS, 1), jnp.float32, 0.0, math.log(10.0)))
    col_scale = jnp.exp(jax.random.uniform(key_cols, (1, D), jnp.float32, math.log(0.5), math.log(2.0)))
    values = jnp.clip(jax.random.normal(key_main, (TOKENS, D), jnp.float32), -3.0, 3.0)
    values = values * row_scale * col_scale
    return values.astype(jnp.bfloat16)


def draw_head_weight(key, part):
    key_main = jax.random.fold_in(key, 2)
    values = jnp.clip(jax.random.normal(key_main, (D, V), jnp.float32) * 0.09375, -0.56, 0.56)
    return values.astype(jnp.bfloat16)


def draw_seq_lengths(key, part):
    key_len, key_pick = jax.random.split(jax.random.fold_in(key, 3))
    lengths = jax.random.randint(key_len, (SEQS,), 1, SEQ_LEN + 1)
    picked = jax.random.randint(key_pick, (), 0, SEQS)
    return jnp.where(jnp.arange(SEQS) == picked, SEQ_LEN, lengths).astype(jnp.int32)


def place_ends(values, rng, least, high):
    place = [jax.random.randint(jax.random.fold_in(rng, axis), (), 0, length) for axis, length in enumerate(values.shape)]
    main_axis = values.shape.index(max(values.shape))
    neighbour = place[:main_axis] + [(place[main_axis] + 1) % values.shape[main_axis]] + place[main_axis + 1:]
    return values.at[tuple(place)].set(least).at[tuple(neighbour)].set(high)


def setup_inputs(seed: int = 0) -> dict:
    keys = jax.random.split(jax.random.key(seed), 6)
    return {
        "hidden": draw_hidden(jax.random.fold_in(keys[5], 71), 0),
        "norm_gain": jnp.clip(1.0 + 0.1 * jax.random.normal(keys[1], (D,), jnp.float32), 0.5, 1.5),
        "head_weight": draw_head_weight(jax.random.fold_in(keys[5], 71), 0),
        "token_ids": place_ends(jax.random.randint(keys[3], (TOKENS,), 0, V), jax.random.fold_in(keys[3], 1), 0, V - 1).astype(jnp.int32),
        "seq_lengths": draw_seq_lengths(jax.random.fold_in(keys[5], 71), 0),
    }


def reference(hidden, norm_gain, head_weight, token_ids, seq_lengths):
    hidden_wide = hidden.astype(jnp.float32)
    mean_square = lax.optimization_barrier(jnp.mean(hidden_wide * hidden_wide, axis=1, keepdims=True))
    normed = (hidden_wide * lax.rsqrt(mean_square + 1e-06) * norm_gain[None, :]).astype(jnp.bfloat16)
    row_index = jnp.arange(TOKENS, dtype=jnp.int32)
    position = row_index % SEQ_LEN
    sequence = row_index // SEQ_LEN
    live_rows = position < seq_lengths[sequence]
    block_rows = normed.reshape(TOKENS // TOK_DEV, TOK_DEV, D)
    block_ids = token_ids.reshape(TOKENS // TOK_DEV, TOK_DEV)

    def block_stats(inputs):
        rows_here, ids_here = inputs
        logits = jnp.dot(rows_here, head_weight, preferred_element_type=jnp.float32)
        largest = lax.optimization_barrier(jnp.max(logits, axis=1, keepdims=True))
        exponent_terms = jnp.exp(logits - largest)
        total_exp = lax.optimization_barrier(jnp.sum(exponent_terms, axis=1))
        log_total = largest[:, 0] + jnp.log(total_exp)
        mean_logit = lax.optimization_barrier(jnp.sum(exponent_terms * logits, axis=1)) / total_exp
        target = jnp.take_along_axis(logits, ids_here[:, None], axis=1)[:, 0]
        return (target - log_total, log_total - mean_logit)
    log_probs, entropies = lax.map(block_stats, (block_rows, block_ids))
    log_probs = jnp.where(live_rows, log_probs.reshape(TOKENS), 0.0)
    entropies = jnp.where(live_rows, entropies.reshape(TOKENS), 0.0)
    return (log_probs, entropies)
```

```python
import functools

import jax
import jax.numpy as jnp
from jax import lax
from jax.experimental import pallas as pl
from jax.experimental.pallas import tpu as pltpu
from jax.sharding import PartitionSpec as P

SEQ_LEN = 2048
EPS = 1e-06
LOW = -1e30
TILE = 256
EXTRA = 16
AXES = ("vocab", "width")
VMEM = pl.BlockSpec(memory_space=pltpu.VMEM)
SMEM = pl.BlockSpec(memory_space=pltpu.SMEM)


class Plan:
    def __init__(self, mesh, rows, columns):
        self.V, self.W = mesh.shape["vocab"], mesh.shape["width"]
        self.X = 1
        while 4 * self.X * self.X <= self.V:
            self.X *= 2
        self.Z = self.V // self.X
        self.rows = rows
        self.part = rows // self.W
        self.blocks = SEQ_LEN // rows
        self.columns = columns

    def perm(self, move):
        return [
            (v * self.W + w, t * self.W + u)
            for v in range(self.V)
            for w in range(self.W)
            for t, u in [move(v, w)]
        ]

    def width_xor(self, k):
        return self.perm(lambda v, w: (v, w ^ k))

    def vocab_xor(self, k):
        return self.perm(lambda v, w: (v ^ k, w))

    def z_ring(self):
        return self.perm(lambda v, w: ((v + self.X) % self.V, w))

    def x_ring(self):
        return self.perm(lambda v, w: (v - v % self.X + (v + 1) % self.X, w))


def quarter(plan, v, w):
    return lax.rem(w + v, plan.W)


def id_rows(plan, ids_ref, w, target):
    out = []
    for h in range(plan.blocks):
        q = quarter(plan, w * plan.blocks + h, target)
        out.append(ids_ref[pl.ds(h * plan.W + q, 1), :])
    return out


def send_kernel(plan, meta_ref, h_ref, gain_ref, ids_ref, *outs):
    v, w = meta_ref[0], meta_ref[1]
    part = plan.part
    gain = gain_ref[...]
    high = gain.astype(jnp.bfloat16).astype(jnp.float32)
    rest = gain - high
    middle = rest.astype(jnp.bfloat16).astype(jnp.float32)
    low = rest - middle
    width = gain.shape[1]
    for k in range(1, plan.W):
        target = w ^ k
        start = pl.multiple_of(quarter(plan, v, target) * part, part)
        outs[k - 1][:part, :] = h_ref[pl.ds(start, part), :]
        rows = [high, middle, low]
        for line in id_rows(plan, ids_ref, w, target):
            upper = line // 256
            for piece in (upper, line - upper * 256):
                piece = piece.astype(jnp.float32)
                if part < width:
                    piece = jnp.concatenate([piece, jnp.zeros((1, width - part), jnp.float32)], axis=1)
                rows.append(piece[:, :width])
        rows.append(jnp.zeros((EXTRA - len(rows), width), jnp.float32))
        outs[k - 1][part:, :] = jnp.concatenate(rows, axis=0).astype(jnp.bfloat16)


def norm_kernel(plan, depth, meta_ref, h_ref, gain_ref, ids_ref, *refs):
    pieces, (out_ref, out_ids) = refs[: plan.W - 1], refs[plan.W - 1 :]
    v, w = meta_ref[0], meta_ref[1]
    part, width = plan.part, gain_ref.shape[1]
    start = pl.multiple_of(quarter(plan, v, w) * part, part)
    wide = [h_ref[pl.ds(start, part), :].astype(jnp.float32)]
    gains = [gain_ref[...]]
    for h, line in enumerate(id_rows(plan, ids_ref, w, w)):
        out_ids[h : h + 1, :] = line
    for k in range(1, plan.W):
        wide.append(pieces[k - 1][:part, :].astype(jnp.float32))
        extra = pieces[k - 1][part:, :].astype(jnp.float32)
        gains.append((extra[0:1] + extra[1:2]) + extra[2:3])
        for h in range(plan.blocks):
            upper = extra[3 + 2 * h : 4 + 2 * h].astype(jnp.int32)
            under = extra[4 + 2 * h : 5 + 2 * h].astype(jnp.int32)
            row = k * plan.blocks + h
            out_ids[row : row + 1, :] = (upper * 256 + under)[:, :part]
    total = sum(jnp.sum(x * x, axis=1, keepdims=True) for x in wide)
    scale = lax.rsqrt(total / depth + EPS)
    for k in range(plan.W):
        normed = (wide[k] * scale * gains[k]).T
        out_ref[k * width : (k + 1) * width, :] = normed.astype(jnp.bfloat16)


def main_kernel(plan, jobs, sizes, bases, have, last, places, meta_ref, seq_ref, ids_ref, *refs):
    refs = list(refs)
    take = lambda n: [refs.pop(0) for _ in range(n)]
    W, part = plan.W, plan.part
    groups = take(len(jobs))
    chunks = [take(W) for _ in sizes]
    offsets = chunk_offsets(plan, sizes, bases, chunks)
    states = [take(1)[0] if h else None for h in have]
    outs = take(4 if last else len(jobs))
    buffers = take(2)
    v, w = meta_ref[0], meta_ref[1]
    z, x = v // plan.X, lax.rem(v, plan.X)
    lane = (8, part)
    for g, mine in enumerate(jobs):
        dz, dx = places[g]
        source = lax.rem(z - dz + plan.Z, plan.Z) * plan.X + lax.rem(x - dx + plan.X, plan.X)
        s, h = source // plan.blocks, lax.rem(source, plan.blocks)
        first = h * plan.rows + quarter(plan, source, w) * part
        live = seq_ref[s] > first
        rank = (s ^ w) * plan.blocks + h

        def run(state):
            ids = jnp.broadcast_to(ids_ref[pl.ds(rank, 1), :], lane)
            ids = ids - lax.broadcasted_iota(jnp.int32, lane, 0) - v * plan.columns

            def dot(c, start, size):
                left = jnp.concatenate(
                    [ref[pl.ds(off + start, size), :] for ref, off in zip(chunks[c], offsets[c])], axis=1
                )
                return jnp.dot(left, groups[g][...], preferred_element_type=jnp.float32)

            def fold(state, buffer, size, base):
                m, e_sum, l_sum, target = state
                n = size // 8
                logits = buffer[:size, :].reshape((n,) + lane)
                top = jnp.maximum(m, jnp.max(logits, axis=0))
                scale = jnp.exp(m - top)
                terms = jnp.exp(logits - top[None])
                e_sum = e_sum * scale + jnp.sum(terms, axis=0)
                l_sum = l_sum * scale + jnp.sum(terms * logits, axis=0)
                there = ids - base
                for i in range(n):
                    target = jnp.where(there == 8 * i, logits[i], target)
                return top, e_sum, l_sum, target

            for c in mine:
                size, base = sizes[c], bases[c]
                full, rest = size // TILE, size % TILE
                if full:
                    buffers[0][...] = dot(c, 0, TILE)

                    def pair(i, state):
                        for j in range(2):
                            at = 2 * i + j
                            buffers[1 - j][...] = dot(c, pl.multiple_of((at + 1) * TILE, TILE), TILE)
                            state = fold(state, buffers[j], TILE, base + at * TILE)
                        return state

                    pairs = (full - 1) // 2
                    state = lax.fori_loop(0, pairs, pair, state)
                    done = 2 * pairs
                    tail = [(a * TILE, TILE) for a in range(done + 1, full)]
                else:
                    done, tail = 0, []
                if rest:
                    tail.append((full * TILE, rest))
                if not full:
                    buffers[0][:rest, :] = dot(c, *tail.pop(0))
                spans = [(done * TILE, TILE if full else rest)] + tail
                for i, (start, count) in enumerate(spans):
                    if i + 1 < len(spans):
                        buffers[1 - i % 2][: spans[i + 1][1], :] = dot(c, *spans[i + 1])
                    state = fold(state, buffers[i % 2], count, base + start)
            return state

        def start_state():
            if have[g]:
                return tuple(states[g][i] for i in range(4))
            zero = jnp.zeros(lane, jnp.float32)
            return jnp.full(lane, LOW, jnp.float32), zero, zero, zero

        state = lax.cond(live, lambda: run(start_state()), start_state)
        if not last:
            for i in range(4):
                outs[g][i] = state[i]
            continue
        m, e_sum, l_sum, target = state
        top = jnp.max(m, axis=0, keepdims=True)
        scale = jnp.exp(m - top)
        lines = [top] + [jnp.sum(a, axis=0, keepdims=True) for a in (e_sum * scale, l_sum * scale, target)]
        for i, line in enumerate(lines):
            outs[i][pl.ds(source, 1), :] = line


def merge(parts):
    top = functools.reduce(jnp.maximum, [p[0] for p in parts])
    scales = [jnp.exp(p[0] - top) for p in parts]
    e_sum = sum(p[1] * c for p, c in zip(parts, scales))
    l_sum = sum(p[2] * c for p, c in zip(parts, scales))
    return top, e_sum, l_sum, sum(p[3] for p in parts)


def merge_kernel(count, *refs):
    parts = [[ref[i] for i in range(4)] for ref in refs[:count]]
    for i, value in enumerate(merge(parts)):
        refs[count][i] = value


def close_kernel(plan, count, meta_ref, *refs):
    parts = [[ref[i] for i in range(4)] for ref in refs[:count]]
    outs, held = refs[count:-1], refs[-1]
    w = meta_ref[1]
    top, e_sum, l_sum, target = merge(parts)
    logsum = top + jnp.log(e_sum)
    held[0] = target - logsum
    held[1] = logsum - l_sum / e_sum
    for k in range(plan.W):
        for h in range(plan.blocks):
            for i in range(2):
                row = i * plan.blocks + h
                outs[k][row : row + 1, :] = held[i, pl.ds((w ^ k) * plan.blocks + h, 1), :]


def place_kernel(plan, meta_ref, seq_ref, *refs):
    pieces, outs = refs[: plan.W], refs[plan.W :]
    w = meta_ref[1]
    length = seq_ref[w]
    column = lax.broadcasted_iota(jnp.int32, (1, plan.part), 1)
    for k in range(plan.W):
        for h in range(plan.blocks):
            q = quarter(plan, w * plan.blocks + h, w ^ k)
            live = column + (h * plan.rows + q * plan.part) < length
            for i in range(2):
                row = i * plan.blocks + h
                outs[i][pl.ds(h * plan.W + q, 1), :] = jnp.where(live, pieces[k][row : row + 1, :], 0.0)


def chunk_offsets(plan, sizes, bases, chunks):
    return [
        [base if ref.shape[0] == plan.columns and size < plan.columns else 0 for ref in refs]
        for size, base, refs in zip(sizes, bases, chunks)
    ]


def call(kernel, out_shape, args, smem, scratch=(), flops=0, name=None):
    return pl.pallas_call(
        kernel,
        out_shape=out_shape,
        in_specs=[SMEM] * smem + [VMEM] * (len(args) - smem),
        out_specs=jax.tree.map(lambda _: VMEM, out_shape),
        scratch_shapes=list(scratch),
        compiler_params=pltpu.CompilerParams(vmem_limit_bytes=24 * 2**20),
        cost_estimate=pl.CostEstimate(flops=flops, bytes_accessed=2**20, transcendentals=0),
        name=name,
    )(*args)


def chunk_spans(columns):
    step = -(-columns // (4 * TILE)) * TILE
    starts = list(range(0, columns, step))
    return [(a, min(step, columns - a)) for a in starts]


def on_device(mesh, hidden, norm_gain, head_weight, token_ids, seq_lengths):
    rows, width = hidden.shape
    columns = head_weight.shape[1]
    plan = Plan(mesh, rows, columns)
    W, part, blocks = plan.W, plan.part, plan.blocks
    depth = width * W
    v = lax.axis_index("vocab").astype(jnp.int32)
    w = lax.axis_index("width").astype(jnp.int32)
    meta = jnp.stack([v, w])
    gain = norm_gain.reshape(1, width)
    ids = token_ids.reshape(blocks * W, part)
    shape = jax.ShapeDtypeStruct
    move = lambda value, perm: lax.ppermute(value, AXES, perm)

    sent = call(
        functools.partial(send_kernel, plan),
        [shape((part + EXTRA, width), jnp.bfloat16)] * (W - 1),
        (meta, hidden, gain, ids),
        1,
        name="send",
    )
    pieces = [move(sent[k - 1], plan.width_xor(k)) for k in range(1, W)]

    spans = chunk_spans(columns)
    weight = head_weight.T
    bits = [1 << i for i in range(W.bit_length() - 1)]
    whole = {0: weight}
    for bit in bits[:1]:
        whole[bit] = move(weight, plan.width_xor(bit))
    chunks = []
    for a, n in spans:
        held = {0: weight[a : a + n]}
        for bit in reversed(bits):
            for k in list(held):
                if (k, bit) != (0, 1):
                    held[k | bit] = move(held[k], plan.width_xor(bit))
        held[0], held[1] = whole[0], whole[1]
        chunks.append([held[k] for k in range(W)])

    normed, all_ids = call(
        functools.partial(norm_kernel, plan, depth),
        [shape((depth, part), jnp.bfloat16), shape((W * blocks, part), jnp.int32)],
        (meta, hidden, gain, ids, *pieces),
        1,
        name="norm",
    )
    groups = {}
    ring = normed
    for dz in range(plan.Z):
        if dz:
            ring = move(ring, plan.z_ring())
        groups[dz, 0] = ring
        for dx in range(1, plan.X):
            groups[dz, dx] = move(groups[dz, dx - 1], plan.x_ring())

    states = {}

    def stage(jobs, last=False):
        keys = list(jobs)
        used = sorted({c for mine in jobs.values() for c in mine})
        have = [key in states for key in keys]
        sizes, bases = [spans[c][1] for c in used], [spans[c][0] for c in used]
        args = [meta, seq_lengths, all_ids] + [groups[key] for key in keys]
        for c in used:
            args += chunks[c]
        args += [states[key] for key in keys if key in states]
        if last:
            out = [shape((plan.V, part), jnp.float32)] * 4
        else:
            out = [shape((4, 8, part), jnp.float32)] * len(keys)
        work = sum(spans[c][1] for mine in jobs.values() for c in mine)
        got = call(
            functools.partial(
                main_kernel, plan, [[used.index(c) for c in jobs[key]] for key in keys], sizes, bases, have, last, keys
            ),
            out,
            args,
            2,
            scratch=[pltpu.VMEM((TILE, part), jnp.float32)] * 2,
            flops=2 * work * part * depth,
            name="logits",
        )
        if last:
            return jnp.stack(got)
        states.update(zip(keys, got))

    stats = stage({key: list(range(len(spans))) for key in groups}, last=True)

    levels = [1 << i for i in range(plan.V.bit_length() - 1)]
    rounds = [levels[i : i + 2] for i in range(0, len(levels), 2)]
    for i, level in enumerate(rounds):
        others = [level[0]] if len(level) == 1 else [level[0], level[1], level[0] | level[1]]
        parts = [stats] + [move(stats, plan.vocab_xor(k)) for k in others]
        if i + 1 < len(rounds):
            stats = call(
                functools.partial(merge_kernel, len(parts)), shape(stats.shape, jnp.float32), parts, 0, name="merge"
            )
    closed = call(
        functools.partial(close_kernel, plan, len(parts)),
        [shape((2 * blocks, part), jnp.float32)] * W,
        (meta, *parts),
        1,
        scratch=[pltpu.VMEM((2, plan.V, part), jnp.float32)],
        name="close",
    )
    closed = [closed[0]] + [move(closed[k], plan.width_xor(k)) for k in range(1, W)]
    log_probs, entropies = call(
        functools.partial(place_kernel, plan),
        [shape((blocks * W, part), jnp.float32)] * 2,
        (meta, seq_lengths, *closed),
        2,
        name="place",
    )
    return log_probs.reshape(-1), entropies.reshape(-1)


def solution(mesh):
    in_specs = (P("vocab", "width"), P("width"), P("width", "vocab"), P("width"), P())
    out_specs = (P("width"), P("width"))
    return jax.shard_map(
        functools.partial(on_device, mesh), mesh=mesh, in_specs=in_specs, out_specs=out_specs, check_vma=False
    )
```

```python
import functools

import jax
import jax.numpy as jnp
from jax import lax
from jax.experimental import pallas as pl
from jax.experimental.pallas import tpu as pltpu
from jax.sharding import PartitionSpec as P

SEQ_LEN = 2048
EPS = 1e-06
LOW = -1e30
TILE = 256
EXTRA = 16
AXES = ("vocab", "width")
VMEM = pl.BlockSpec(memory_space=pltpu.VMEM)
SMEM = pl.BlockSpec(memory_space=pltpu.SMEM)
HBM = pl.BlockSpec(memory_space=pltpu.HBM)


class Plan:
    def __init__(self, mesh, rows, columns):
        self.V, self.W = mesh.shape["vocab"], mesh.shape["width"]
        self.X = 1
        while 4 * self.X * self.X <= self.V:
            self.X *= 2
        self.Z = self.V // self.X
        self.rows = rows
        self.part = rows // self.W
        self.blocks = SEQ_LEN // rows
        self.columns = columns

    def perm(self, move):
        return [
            (v * self.W + w, t * self.W + u)
            for v in range(self.V)
            for w in range(self.W)
            for t, u in [move(v, w)]
        ]

    def width_xor(self, k):
        return self.perm(lambda v, w: (v, w ^ k))

    def vocab_xor(self, k):
        return self.perm(lambda v, w: (v ^ k, w))

    def z_ring(self):
        return self.perm(lambda v, w: ((v + self.X) % self.V, w))

    def x_ring(self):
        return self.perm(lambda v, w: (v - v % self.X + (v + 1) % self.X, w))


def quarter(plan, v, w):
    return lax.rem(w + v, plan.W)


def id_rows(plan, ids_ref, w, target):
    out = []
    for h in range(plan.blocks):
        q = quarter(plan, w * plan.blocks + h, target)
        start = pl.multiple_of((h * plan.W + q) * plan.part, plan.part)
        out.append(ids_ref[pl.ds(start, plan.part)].reshape(1, plan.part))
    return out


def send_kernel(plan, h_ref, gain_hbm, ids_hbm, *refs):
    outs, (gain_ref, ids_ref, sems) = refs[: plan.W], refs[plan.W :]
    v, w = lax.axis_index("vocab"), lax.axis_index("width")
    part = plan.part
    small = [
        pltpu.make_async_copy(gain_hbm, gain_ref, sems.at[0]),
        pltpu.make_async_copy(ids_hbm, ids_ref, sems.at[1]),
    ]
    for copy in small:
        copy.start()
    large = []
    for k in range(plan.W):
        start = pl.multiple_of(quarter(plan, v, w ^ k) * part, part)
        large.append(pltpu.make_async_copy(h_ref.at[pl.ds(start, part)], outs[k].at[pl.ds(0, part)], sems.at[2 + k]))
        large[-1].start()
    for copy in small:
        copy.wait()
    gain = gain_ref[...].reshape(1, gain_ref.shape[0])
    high = gain.astype(jnp.bfloat16).astype(jnp.float32)
    rest = gain - high
    middle = rest.astype(jnp.bfloat16).astype(jnp.float32)
    low = rest - middle
    width = gain.shape[1]
    for k in range(plan.W):
        rows = [high, middle, low]
        for line in id_rows(plan, ids_ref, w, w ^ k):
            upper = line // 256
            for piece in (upper, line - upper * 256):
                piece = piece.astype(jnp.float32)
                if part < width:
                    piece = jnp.concatenate([piece, jnp.zeros((1, width - part), jnp.float32)], axis=1)
                rows.append(piece[:, :width])
        rows.append(jnp.zeros((EXTRA - len(rows), width), jnp.float32))
        outs[k][part:, :] = jnp.concatenate(rows, axis=0).astype(jnp.bfloat16)
    for copy in large:
        copy.wait()


def norm_kernel(plan, depth, *refs):
    pieces, (out_ref, out_ids) = refs[: plan.W], refs[plan.W :]
    part, width = plan.part, depth // plan.W
    wide, gains = [], []
    for k in range(plan.W):
        wide.append(pieces[k][:part, :].astype(jnp.float32))
        extra = pieces[k][part:, :].astype(jnp.float32)
        gains.append((extra[0:1] + extra[1:2]) + extra[2:3])
        for h in range(plan.blocks):
            upper = extra[3 + 2 * h : 4 + 2 * h].astype(jnp.int32)
            under = extra[4 + 2 * h : 5 + 2 * h].astype(jnp.int32)
            row = k * plan.blocks + h
            out_ids[row : row + 1, :] = (upper * 256 + under)[:, :part]
    total = sum(jnp.sum(x * x, axis=1, keepdims=True) for x in wide)
    scale = lax.rsqrt(total / depth + EPS)
    for k in range(plan.W):
        normed = (wide[k] * scale * gains[k]).T
        out_ref[k * width : (k + 1) * width, :] = normed.astype(jnp.bfloat16)


def main_kernel(plan, jobs, sizes, bases, have, last, places, halves, where, offsets, seq_ref, ids_ref, *refs):
    refs = list(refs)
    take = lambda n: [refs.pop(0) for _ in range(n)]
    W, part = plan.W, plan.part
    groups = [take(n) for n in halves]
    held = take(max(where) + 1)
    chunks = [[held[i] for i in where[c * W : (c + 1) * W]] for c in range(len(sizes))]
    states = [take(1)[0] if h else None for h in have]
    outs = take(1 if last else len(jobs))
    buffers = take(2)
    v, w = lax.axis_index("vocab"), lax.axis_index("width")
    z, x = v // plan.X, lax.rem(v, plan.X)
    lane = (8, part)
    for g, mine in enumerate(jobs):
        dz, dx = places[g]
        source = lax.rem(z - dz + plan.Z, plan.Z) * plan.X + lax.rem(x - dx + plan.X, plan.X)
        s, h = source // plan.blocks, lax.rem(source, plan.blocks)
        first = h * plan.rows + quarter(plan, source, w) * part
        live = seq_ref[s] > first
        rank = (s ^ w) * plan.blocks + h

        def run(state):
            ids = jnp.broadcast_to(ids_ref[pl.ds(rank, 1), :], lane)
            ids = ids - lax.broadcasted_iota(jnp.int32, lane, 0) - v * plan.columns

            def right():
                held = [ref[...] for ref in groups[g]]
                return held[0] if len(held) == 1 else jnp.concatenate(held, axis=0)

            def dot(c, start, size):
                left = jnp.concatenate(
                    [ref[off + start : off + start + size, :] for ref, off in zip(chunks[c], offsets[c])], axis=1
                )
                return jnp.dot(left, right(), preferred_element_type=jnp.float32)

            def fold(state, buffer, size, base):
                m, e_sum, l_sum, target = state
                n = size // 8
                logits = buffer[:size, :].reshape((n,) + lane)
                top = jnp.maximum(m, jnp.max(logits, axis=0))
                scale = jnp.exp(m - top)
                terms = jnp.exp(logits - top[None])
                e_sum = e_sum * scale + jnp.sum(terms, axis=0)
                l_sum = l_sum * scale + jnp.sum(terms * logits, axis=0)
                there = ids - base
                for i in range(n):
                    target = jnp.where(there == 8 * i, logits[i], target)
                return top, e_sum, l_sum, target

            tiles = [(c, at, min(TILE, sizes[c] - at)) for c in mine for at in range(0, sizes[c], TILE)]
            buffers[0][: tiles[0][2], :] = dot(*tiles[0])
            for i, (c, at, size) in enumerate(tiles):
                if i + 1 < len(tiles):
                    buffers[1 - i % 2][: tiles[i + 1][2], :] = dot(*tiles[i + 1])
                state = fold(state, buffers[i % 2], size, bases[c] + at)
            return state

        def start_state():
            if have[g]:
                return tuple(states[g][i] for i in range(4))
            zero = jnp.zeros(lane, jnp.float32)
            return jnp.full(lane, LOW, jnp.float32), zero, zero, zero

        state = lax.cond(live, lambda: run(start_state()), start_state) if mine else start_state()
        if not last:
            for i in range(4):
                outs[g][i] = state[i]
            continue
        m, e_sum, l_sum, target = state
        top = jnp.max(m, axis=0, keepdims=True)
        scale = jnp.exp(m - top)
        lines = [top] + [jnp.sum(a, axis=0, keepdims=True) for a in (e_sum * scale, l_sum * scale, target)]
        for i, line in enumerate(lines):
            outs[0][i, pl.ds(source, 1), :] = line


def merge(parts):
    top = functools.reduce(jnp.maximum, [p[0] for p in parts])
    scales = [jnp.exp(p[0] - top) for p in parts]
    e_sum = sum(p[1] * c for p, c in zip(parts, scales))
    l_sum = sum(p[2] * c for p, c in zip(parts, scales))
    return top, e_sum, l_sum, sum(p[3] for p in parts)


def read(ref):
    return [ref[i] for i in range(4)]


def results(stats):
    top, e_sum, l_sum, target = stats
    logsum = top + jnp.log(e_sum)
    return target - logsum, logsum - l_sum / e_sum


def merge_kernel(count, *refs):
    for i, value in enumerate(merge([read(ref) for ref in refs[:count]])):
        refs[count][i] = value


def split_kernel(plan, count, *refs):
    mine, other = refs[count:]
    upper = lax.axis_index("width") // 2 == 1
    half = plan.V // 2
    for i, value in enumerate(merge([read(ref) for ref in refs[:count]])):
        mine[i] = jnp.where(upper, value[half:], value[:half])
        other[i] = jnp.where(upper, value[:half], value[half:])


def pair_kernel(plan, a_ref, b_ref, c_ref, d_ref, keep_ref, pass_ref):
    odd = lax.rem(lax.axis_index("width"), 2) == 1
    blocks = plan.blocks
    for n, (one, two) in enumerate(((a_ref, b_ref), (c_ref, d_ref))):
        for i, value in enumerate(results(merge([read(one), read(two)]))):
            rows = slice((2 * n + i) * blocks, (2 * n + i + 1) * blocks)
            keep_ref[rows, :] = jnp.where(odd, value[blocks:], value[:blocks])
            pass_ref[rows, :] = jnp.where(odd, value[:blocks], value[blocks:])


def close_kernel(plan, count, *refs):
    outs, held = refs[count:-1], refs[-1]
    w = lax.axis_index("width")
    for i, value in enumerate(results(merge([read(ref) for ref in refs[:count]]))):
        held[i] = value
    for k in range(plan.W):
        for h in range(plan.blocks):
            for i in range(2):
                row = i * plan.blocks + h
                outs[k][row : row + 1, :] = held[i, pl.ds((w ^ k) * plan.blocks + h, 1), :]


def place_kernel(plan, count, order, seq_ref, *refs):
    pieces, outs = refs[:count], refs[count:]
    w = lax.axis_index("width")
    length = seq_ref[w]
    column = lax.broadcasted_iota(jnp.int32, (1, plan.part), 1)
    sets = len(order) // count
    for n, k in enumerate(order):
        for h in range(plan.blocks):
            q = quarter(plan, w * plan.blocks + h, w ^ k)
            live = column + (h * plan.rows + q * plan.part) < length
            start = pl.multiple_of((h * plan.W + q) * plan.part, plan.part)
            for i in range(2):
                row = (2 * (n % sets) + i) * plan.blocks + h
                value = jnp.where(live, pieces[n // sets][row : row + 1, :], 0.0)
                outs[i][pl.ds(start, plan.part)] = value.reshape(plan.part)


def call(kernel, out_shape, args, smem, scratch=(), flops=0, name=None, far=0, limit=12):
    return pl.pallas_call(
        kernel,
        out_shape=out_shape,
        in_specs=[SMEM] * smem + [HBM] * far + [VMEM] * (len(args) - smem - far),
        out_specs=jax.tree.map(lambda _: VMEM, out_shape),
        scratch_shapes=list(scratch),
        compiler_params=pltpu.CompilerParams(vmem_limit_bytes=limit * 2**20),
        cost_estimate=pl.CostEstimate(flops=flops, bytes_accessed=2**20, transcendentals=0),
        name=name,
    )(*args)


def chunk_spans(columns, shares=(0.32, 0.64)):
    ends = [0] + [TILE * round(columns * share / TILE) for share in shares] + [columns]
    return [(a, b - a) for a, b in zip(ends, ends[1:])]


def tie(*values):
    return lax.optimization_barrier(values)


def on_device(mesh, hidden, norm_gain, head_weight, token_ids, seq_lengths):
    rows, width = hidden.shape
    columns = head_weight.shape[1]
    plan = Plan(mesh, rows, columns)
    W, part, blocks = plan.W, plan.part, plan.blocks
    depth = width * W
    shape = jax.ShapeDtypeStruct
    move = lambda value, perm: lax.ppermute(value, AXES, perm)

    sent = call(
        functools.partial(send_kernel, plan),
        [shape((part + EXTRA, width), jnp.bfloat16)] * W,
        (hidden, norm_gain, token_ids),
        0,
        scratch=[
            pltpu.VMEM((width,), jnp.float32),
            pltpu.VMEM(token_ids.shape, jnp.int32),
            pltpu.SemaphoreType.DMA((2 + W,)),
        ],
        name="send",
        far=3,
        limit=56,
    )
    pieces = {k: move(sent[k], plan.width_xor(k)) for k in sorted(range(1, W), key=lambda k: (k != 1, -k))}
    pieces = [sent[0]] + [pieces[k] for k in range(1, W)]
    normed, all_ids = call(
        functools.partial(norm_kernel, plan, depth),
        [shape((depth, part), jnp.bfloat16), shape((W * blocks, part), jnp.int32)],
        pieces,
        0,
        name="norm",
    )

    spans = chunk_spans(columns)
    weight = head_weight.T
    bits = [1 << i for i in range(W.bit_length() - 1)]
    near = move(weight, plan.width_xor(1))

    def far_chunk(c, after):
        a, n = spans[c]
        held = {0: tie(weight[a : a + n], *after)[0]}
        for bit in reversed(bits[1:]):
            for k in list(held):
                held[k | bit] = move(held[k], plan.width_xor(bit))
        return held

    def near_chunk(c, held):
        start, size = spans[c]
        cut = size // 32 * 16
        for at, count in ((0, cut), (cut, size - cut)):
            refs = {0: (weight, start + at), 1: (near, start + at)}
            for k in held:
                if k:
                    refs[k] = (held[k], at)
                    refs[k | 1] = (move(held[k][at : at + count], plan.width_xor(1)), 0)
            chunks.append([refs[k] for k in range(W)])
            parts.append((start + at, count))

    states, groups, chunks, parts, done = {}, {}, [], [], {}

    def stage(wanted, last=False):
        jobs = {key: [c for c in mine if c not in done.get(key, [])] for key, mine in wanted.items()}
        done.update(wanted)
        keys = list(jobs)
        used = sorted({c for mine in jobs.values() for c in mine})
        have = [key in states for key in keys]
        sizes, bases = [parts[c][1] for c in used], [parts[c][0] for c in used]
        args = [seq_lengths, all_ids] + [part for key in keys if jobs[key] for part in groups[key]]
        halves = [len(groups[key]) if jobs[key] else 0 for key in keys]
        held = [chunks[c][k][0] for c in used for k in range(W)]
        offsets = [[chunks[c][k][1] for k in range(W)] for c in used]
        unique = [held[i] for i in range(len(held)) if all(held[i] is not held[j] for j in range(i))]
        where = [next(j for j in range(len(unique)) if unique[j] is one) for one in held]
        args += unique
        args += [states[key] for key in keys if key in states]
        if last:
            out = [shape((4, plan.V, part), jnp.float32)]
        else:
            out = [shape((4, 8, part), jnp.float32)] * len(keys)
        work = sum(parts[c][1] for mine in jobs.values() for c in mine)
        got = call(
            functools.partial(
                main_kernel, plan, [[used.index(c) for c in jobs[key]] for key in keys], sizes, bases, have, last, keys,
                halves, where,
                offsets
            ),
            out,
            args,
            1,
            scratch=[pltpu.VMEM((TILE, part), jnp.float32)] * 2,
            flops=2 * work * part * depth,
            name="logits",
        )
        if last:
            return got[0]
        states.update(zip(keys, got))

    groups[0, 0] = [normed]
    ring, far = normed, {}
    fast = plan.X == 2 and plan.Z == 4
    for dz in range(plan.Z):
        end = dz == plan.Z - 1
        onward, arrived, tied = [], {}, {}
        if not end:
            onward = [move(ring, plan.z_ring())]
        if end and plan.X == 2:
            half = depth // 2
            arrived[dz, 1] = [
                move(ring[:half], plan.x_ring()),
                move(groups[dz - 1, 1][0][half:], plan.z_ring()),
            ]
        else:
            passed = ring
            for dx in range(1, plan.X):
                passed = move(passed, plan.x_ring())
                arrived[dz, dx] = [passed]
        if dz < len(spans):
            tied["far"] = far_chunk(dz, pieces[-1:])
        if far:
            near_chunk(dz - 1, far)
            if fast:
                stage({key: list(range(len(chunks))) for key in groups})
                tied["states"] = states
        onward, arrived, tied = lax.optimization_barrier((onward, arrived, tied))
        states = tied.get("states", states)
        far = tied.get("far", {})
        groups.update(arrived)
        if not end:
            ring = onward[0]
            groups[dz + 1, 0] = onward
    stats = stage({key: list(range(len(chunks))) for key in groups}, last=True)

    levels = [1 << i for i in range(plan.V.bit_length() - 1)]
    if W == 4 and plan.V == 8:
        parts = [stats] + [move(stats, plan.vocab_xor(k)) for k in (1, 2, 3)]
        mine, other = call(
            functools.partial(split_kernel, plan, 4),
            [shape((4, plan.V // 2, part), jnp.float32)] * 2,
            parts,
            0,
            name="split",
        )
        arrived = [
            move(other, plan.width_xor(2)),
            move(mine, plan.vocab_xor(4)),
            move(other, plan.perm(lambda v, w: (v ^ 4, w ^ 2))),
        ]
        keep, passed = call(
            functools.partial(pair_kernel, plan),
            [shape((4 * blocks, part), jnp.float32)] * 2,
            (mine, arrived[1], arrived[0], arrived[2]),
            0,
            name="pair",
        )
        closed, order = [keep, move(passed, plan.width_xor(1))], (0, 2, 1, 3)
    else:
        rounds = [levels[i : i + 2] for i in range(0, len(levels), 2)]
        for i, level in enumerate(rounds):
            others = [level[0]] if len(level) == 1 else [level[0], level[1], level[0] | level[1]]
            parts = [stats] + [move(stats, plan.vocab_xor(k)) for k in others]
            if i + 1 < len(rounds):
                stats = call(
                    functools.partial(merge_kernel, len(parts)), shape(stats.shape, jnp.float32), parts, 0, name="merge"
                )
        closed = call(
            functools.partial(close_kernel, plan, len(parts)),
            [shape((2 * blocks, part), jnp.float32)] * W,
            parts,
            0,
            scratch=[pltpu.VMEM((2, plan.V, part), jnp.float32)],
            name="close",
        )
        closed = [closed[0]] + [move(closed[k], plan.width_xor(k)) for k in range(1, W)]
        order = tuple(range(W))
    return tuple(
        call(
            functools.partial(place_kernel, plan, len(closed), order),
            [shape(token_ids.shape, jnp.float32)] * 2,
            (seq_lengths, *closed),
            1,
            name="place",
        )
    )


def solution(mesh):
    in_specs = (P("vocab", "width"), P("width"), P("width", "vocab"), P("width"), P())
    out_specs = (P("width"), P("width"))
    return jax.shard_map(
        functools.partial(on_device, mesh), mesh=mesh, in_specs=in_specs, out_specs=out_specs, check_vma=False
    )
```

```python
import functools

import jax
import jax.numpy as jnp
from jax import lax
from jax.experimental import pallas as pl
from jax.experimental.pallas import tpu as pltpu
from jax.sharding import PartitionSpec as P

SEQ_LEN = 2048
EPS = 1e-06
LOW = -1e30
TILE = 256
EXTRA = 16
NEAR = 1024
AXES = ("vocab", "width")
VMEM = pl.BlockSpec(memory_space=pltpu.VMEM)
SMEM = pl.BlockSpec(memory_space=pltpu.SMEM)
HBM = pl.BlockSpec(memory_space=pltpu.HBM)


class Plan:
    def __init__(self, mesh, rows, columns):
        self.V, self.W = mesh.shape["vocab"], mesh.shape["width"]
        self.X = 1
        while 4 * self.X * self.X <= self.V:
            self.X *= 2
        self.Z = self.V // self.X
        self.rows = rows
        self.part = rows // self.W
        self.blocks = SEQ_LEN // rows
        self.columns = columns

    def perm(self, move):
        return [
            (v * self.W + w, t * self.W + u)
            for v in range(self.V)
            for w in range(self.W)
            for t, u in [move(v, w)]
        ]

    def width_xor(self, k):
        return self.perm(lambda v, w: (v, w ^ k))

    def vocab_xor(self, k):
        return self.perm(lambda v, w: (v ^ k, w))

    def z_ring(self):
        return self.perm(lambda v, w: ((v + self.X) % self.V, w))

    def x_ring(self):
        return self.perm(lambda v, w: (v - v % self.X + (v + 1) % self.X, w))


def quarter(plan, v, w):
    return lax.rem(w + v, plan.W)


def id_rows(plan, ids_ref, w, target):
    out = []
    for h in range(plan.blocks):
        q = quarter(plan, w * plan.blocks + h, target)
        start = pl.multiple_of((h * plan.W + q) * plan.part, plan.part)
        out.append(ids_ref[pl.ds(start, plan.part)].reshape(1, plan.part))
    return out


def send_kernel(plan, h_ref, gain_hbm, ids_hbm, *refs):
    outs, (gain_ref, ids_ref, sems) = refs[: plan.W], refs[plan.W :]
    v, w = lax.axis_index("vocab"), lax.axis_index("width")
    part = plan.part
    small = [
        pltpu.make_async_copy(gain_hbm, gain_ref, sems.at[0]),
        pltpu.make_async_copy(ids_hbm, ids_ref, sems.at[1]),
    ]
    for copy in small:
        copy.start()
    large = []
    for k in range(plan.W):
        start = pl.multiple_of(quarter(plan, v, w ^ k) * part, part)
        large.append(pltpu.make_async_copy(h_ref.at[pl.ds(start, part)], outs[k].at[pl.ds(0, part)], sems.at[2 + k]))
        large[-1].start()
    for copy in small:
        copy.wait()
    gain = gain_ref[...].reshape(1, gain_ref.shape[0])
    high = gain.astype(jnp.bfloat16).astype(jnp.float32)
    rest = gain - high
    middle = rest.astype(jnp.bfloat16).astype(jnp.float32)
    low = rest - middle
    width = gain.shape[1]
    for k in range(plan.W):
        rows = [high, middle, low]
        for line in id_rows(plan, ids_ref, w, w ^ k):
            upper = line // 256
            for piece in (upper, line - upper * 256):
                piece = piece.astype(jnp.float32)
                if part < width:
                    piece = jnp.concatenate([piece, jnp.zeros((1, width - part), jnp.float32)], axis=1)
                rows.append(piece[:, :width])
        rows.append(jnp.zeros((EXTRA - len(rows), width), jnp.float32))
        outs[k][part:, :] = jnp.concatenate(rows, axis=0).astype(jnp.bfloat16)
    for copy in large:
        copy.wait()


def norm_kernel(plan, depth, *refs):
    pieces, (out_ref, out_ids) = refs[: plan.W], refs[plan.W :]
    part, width = plan.part, depth // plan.W
    wide, gains = [], []
    for k in range(plan.W):
        wide.append(pieces[k][:part, :].astype(jnp.float32))
        extra = pieces[k][part:, :].astype(jnp.float32)
        gains.append((extra[0:1] + extra[1:2]) + extra[2:3])
        for h in range(plan.blocks):
            upper = extra[3 + 2 * h : 4 + 2 * h].astype(jnp.int32)
            under = extra[4 + 2 * h : 5 + 2 * h].astype(jnp.int32)
            row = k * plan.blocks + h
            out_ids[row : row + 1, :] = (upper * 256 + under)[:, :part]
    total = sum(jnp.sum(x * x, axis=1, keepdims=True) for x in wide)
    scale = lax.rsqrt(total / depth + EPS)
    for k in range(plan.W):
        normed = (wide[k] * scale * gains[k]).T
        out_ref[k * width : (k + 1) * width, :] = normed.astype(jnp.bfloat16)


def main_kernel(plan, jobs, sizes, bases, have, last, places, halves, where, offsets, seq_ref, ids_ref, *refs):
    refs = list(refs)
    take = lambda n: [refs.pop(0) for _ in range(n)]
    W, part = plan.W, plan.part
    groups = [take(n) for n in halves]
    held = take(max(where) + 1)
    chunks = [[held[i] for i in where[c * W : (c + 1) * W]] for c in range(len(sizes))]
    states = [take(1)[0] if h else None for h in have]
    outs = take(1 if last else len(jobs))
    buffers = take(2)
    v, w = lax.axis_index("vocab"), lax.axis_index("width")
    z, x = v // plan.X, lax.rem(v, plan.X)
    lane = (8, part)
    for g, mine in enumerate(jobs):
        dz, dx = places[g]
        source = lax.rem(z - dz + plan.Z, plan.Z) * plan.X + lax.rem(x - dx + plan.X, plan.X)
        s, h = source // plan.blocks, lax.rem(source, plan.blocks)
        first = h * plan.rows + quarter(plan, source, w) * part
        live = seq_ref[s] > first
        rank = (s ^ w) * plan.blocks + h

        def run(state):
            ids = jnp.broadcast_to(ids_ref[pl.ds(rank, 1), :], lane)
            ids = ids - lax.broadcasted_iota(jnp.int32, lane, 0) - v * plan.columns

            def right():
                held = [ref[...] for ref in groups[g]]
                return held[0] if len(held) == 1 else jnp.concatenate(held, axis=0)

            def dot(c, start, size):
                left = jnp.concatenate(
                    [ref[off + start : off + start + size, :] for ref, off in zip(chunks[c], offsets[c])], axis=1
                )
                return jnp.dot(left, right(), preferred_element_type=jnp.float32)

            def fold(state, buffer, size, base):
                m, e_sum, l_sum, target = state
                n = size // 8
                logits = buffer[:size, :].reshape((n,) + lane)
                top = jnp.maximum(m, jnp.max(logits, axis=0))
                scale = jnp.exp(m - top)
                terms = jnp.exp(logits - top[None])
                e_sum = e_sum * scale + jnp.sum(terms, axis=0)
                l_sum = l_sum * scale + jnp.sum(terms * logits, axis=0)
                there = ids - base
                for i in range(n):
                    target = jnp.where(there == 8 * i, logits[i], target)
                return top, e_sum, l_sum, target

            tiles = [(c, at, size) for c in mine for at, size in even(sizes[c], TILE)]
            buffers[0][: tiles[0][2], :] = dot(*tiles[0])
            for i, (c, at, size) in enumerate(tiles):
                if i + 1 < len(tiles):
                    buffers[1 - i % 2][: tiles[i + 1][2], :] = dot(*tiles[i + 1])
                state = fold(state, buffers[i % 2], size, bases[c] + at)
            return state

        def start_state():
            if have[g]:
                return tuple(states[g][i] for i in range(4))
            zero = jnp.zeros(lane, jnp.float32)
            return jnp.full(lane, LOW, jnp.float32), zero, zero, zero

        state = lax.cond(live, lambda: run(start_state()), start_state) if mine else start_state()
        if not last:
            for i in range(4):
                outs[g][i] = state[i]
            continue
        m, e_sum, l_sum, target = state
        top = jnp.max(m, axis=0, keepdims=True)
        scale = jnp.exp(m - top)
        lines = [top] + [jnp.sum(a, axis=0, keepdims=True) for a in (e_sum * scale, l_sum * scale, target)]
        for i, line in enumerate(lines):
            outs[0][i, pl.ds(source, 1), :] = line


def merge(parts):
    top = functools.reduce(jnp.maximum, [p[0] for p in parts])
    scales = [jnp.exp(p[0] - top) for p in parts]
    e_sum = sum(p[1] * c for p, c in zip(parts, scales))
    l_sum = sum(p[2] * c for p, c in zip(parts, scales))
    return top, e_sum, l_sum, sum(p[3] for p in parts)


def read(ref):
    return [ref[i] for i in range(4)]


def results(stats):
    top, e_sum, l_sum, target = stats
    logsum = top + jnp.log(e_sum)
    return target - logsum, logsum - l_sum / e_sum


def merge_kernel(count, *refs):
    for i, value in enumerate(merge([read(ref) for ref in refs[:count]])):
        refs[count][i] = value


def split_kernel(plan, count, *refs):
    mine, other = refs[count:]
    upper = lax.axis_index("width") // 2 == 1
    half = plan.V // 2
    for i, value in enumerate(merge([read(ref) for ref in refs[:count]])):
        mine[i] = jnp.where(upper, value[half:], value[:half])
        other[i] = jnp.where(upper, value[:half], value[half:])


def pair_kernel(plan, d_ref, b_ref, c_ref, a_ref, keep_ref, pass_ref):
    odd = lax.rem(lax.axis_index("width"), 2) == 1
    blocks = plan.blocks
    for n, (one, two) in enumerate(((a_ref, b_ref), (c_ref, d_ref))):
        for i, value in enumerate(results(merge([read(one), read(two)]))):
            rows = slice((2 * n + i) * blocks, (2 * n + i + 1) * blocks)
            keep_ref[rows, :] = jnp.where(odd, value[blocks:], value[:blocks])
            pass_ref[rows, :] = jnp.where(odd, value[:blocks], value[blocks:])


def close_kernel(plan, count, *refs):
    outs, held = refs[count:-1], refs[-1]
    w = lax.axis_index("width")
    for i, value in enumerate(results(merge([read(ref) for ref in refs[:count]]))):
        held[i] = value
    for k in range(plan.W):
        for h in range(plan.blocks):
            for i in range(2):
                row = i * plan.blocks + h
                outs[k][row : row + 1, :] = held[i, pl.ds((w ^ k) * plan.blocks + h, 1), :]


def place_kernel(plan, count, order, seq_ref, *refs):
    pieces, outs = refs[:count], refs[count:]
    w = lax.axis_index("width")
    length = seq_ref[w]
    column = lax.broadcasted_iota(jnp.int32, (1, plan.part), 1)
    sets = len(order) // count
    for n, k in enumerate(order):
        for h in range(plan.blocks):
            q = quarter(plan, w * plan.blocks + h, w ^ k)
            live = column + (h * plan.rows + q * plan.part) < length
            start = pl.multiple_of((h * plan.W + q) * plan.part, plan.part)
            for i in range(2):
                row = (2 * (n % sets) + i) * plan.blocks + h
                value = jnp.where(live, pieces[n // sets][row : row + 1, :], 0.0)
                outs[i][pl.ds(start, plan.part)] = value.reshape(plan.part)


def call(kernel, out_shape, args, smem, scratch=(), flops=0, name=None, far=0, limit=12):
    return pl.pallas_call(
        kernel,
        out_shape=out_shape,
        in_specs=[SMEM] * smem + [HBM] * far + [VMEM] * (len(args) - smem - far),
        out_specs=jax.tree.map(lambda _: VMEM, out_shape),
        scratch_shapes=list(scratch),
        compiler_params=pltpu.CompilerParams(vmem_limit_bytes=limit * 2**20),
        cost_estimate=pl.CostEstimate(flops=flops, bytes_accessed=2**20, transcendentals=0),
        name=name,
    )(*args)


def chunk_spans(columns, shares=(0.32, 0.733)):
    ends = [0] + [64 * round(columns * share / 64) for share in shares] + [columns]
    return [(a, b - a) for a, b in zip(ends, ends[1:])]


def even(size, most):
    step = -(-size // (16 * -(-size // most))) * 16
    return [(at, min(step, size - at)) for at in range(0, size, step)]


def tie(*values):
    return lax.optimization_barrier(values)


def on_device(mesh, hidden, norm_gain, head_weight, token_ids, seq_lengths):
    rows, width = hidden.shape
    columns = head_weight.shape[1]
    plan = Plan(mesh, rows, columns)
    W, part, blocks = plan.W, plan.part, plan.blocks
    depth = width * W
    shape = jax.ShapeDtypeStruct
    move = lambda value, perm: lax.ppermute(value, AXES, perm)

    sent = call(
        functools.partial(send_kernel, plan),
        [shape((part + EXTRA, width), jnp.bfloat16)] * W,
        [pltpu.with_memory_space_constraint(x, pltpu.HBM) for x in (hidden, norm_gain, token_ids)],
        0,
        scratch=[
            pltpu.VMEM((width,), jnp.float32),
            pltpu.VMEM(token_ids.shape, jnp.int32),
            pltpu.SemaphoreType.DMA((2 + W,)),
        ],
        name="send",
        far=3,
    )
    pieces = {k: move(sent[k], plan.width_xor(k)) for k in sorted(range(1, W), key=lambda k: (k != 1, -k))}
    pieces = [sent[0]] + [pieces[k] for k in range(1, W)]
    normed, all_ids = call(
        functools.partial(norm_kernel, plan, depth),
        [shape((depth, part), jnp.bfloat16), shape((W * blocks, part), jnp.int32)],
        pieces,
        0,
        name="norm",
    )

    spans = chunk_spans(columns)
    weight = head_weight.T
    bits = [1 << i for i in range(W.bit_length() - 1)]
    near = move(weight, plan.width_xor(1))

    def far_chunk(c, after):
        a, n = spans[c]
        held = {0: tie(weight[a : a + n], *after)[0]}
        for bit in reversed(bits[1:]):
            for k in list(held):
                held[k | bit] = move(held[k], plan.width_xor(bit))
        return held

    def near_chunk(c, held):
        start, size = spans[c]
        for at, count in even(size, NEAR):
            refs = {0: (weight, start + at), 1: (near, start + at)}
            for k in held:
                if k:
                    refs[k] = (held[k], at)
                    refs[k | 1] = (move(held[k][at : at + count], plan.width_xor(1)), 0)
            chunks.append([refs[k] for k in range(W)])
            parts.append((start + at, count))

    states, groups, chunks, parts, done = {}, {}, [], [], {}

    def stage(wanted, last=False):
        jobs = {key: [c for c in mine if c not in done.get(key, [])] for key, mine in wanted.items()}
        done.update(wanted)
        keys = list(jobs)
        used = sorted({c for mine in jobs.values() for c in mine})
        have = [key in states for key in keys]
        sizes, bases = [parts[c][1] for c in used], [parts[c][0] for c in used]
        args = [seq_lengths, all_ids] + [part for key in keys if jobs[key] for part in groups[key]]
        halves = [len(groups[key]) if jobs[key] else 0 for key in keys]
        held = [chunks[c][k][0] for c in used for k in range(W)]
        offsets = [[chunks[c][k][1] for k in range(W)] for c in used]
        unique = [held[i] for i in range(len(held)) if all(held[i] is not held[j] for j in range(i))]
        where = [next(j for j in range(len(unique)) if unique[j] is one) for one in held]
        args += unique
        args += [states[key] for key in keys if key in states]
        if last:
            out = [shape((4, plan.V, part), jnp.float32)]
        else:
            out = [shape((4, 8, part), jnp.float32)] * len(keys)
        work = sum(parts[c][1] for mine in jobs.values() for c in mine)
        got = call(
            functools.partial(
                main_kernel, plan, [[used.index(c) for c in jobs[key]] for key in keys], sizes, bases, have, last, keys,
                halves, where,
                offsets
            ),
            out,
            args,
            1,
            scratch=[pltpu.VMEM((TILE, part), jnp.float32)] * 2,
            flops=2 * work * part * depth,
            name="logits",
        )
        if last:
            return got[0]
        states.update(zip(keys, got))

    groups[0, 0] = [normed]
    ring, far = normed, {}
    fast = plan.X == 2 and plan.Z == 4
    for dz in range(plan.Z):
        end = dz == plan.Z - 1
        onward, arrived, tied = [], {}, {}
        if not end:
            onward = [move(ring, plan.z_ring())]
        if end and plan.X == 2:
            half = depth // 2
            arrived[dz, 1] = [
                move(ring[:half], plan.x_ring()),
                move(groups[dz - 1, 1][0][half:], plan.z_ring()),
            ]
        else:
            passed = ring
            for dx in range(1, plan.X):
                passed = move(passed, plan.x_ring())
                arrived[dz, dx] = [passed]
        if dz < len(spans):
            tied["far"] = far_chunk(dz, pieces[-1:])
        if far:
            near_chunk(dz - 1, far)
            if fast:
                stage({key: list(range(len(chunks))) for key in groups})
                tied["states"] = states
        onward, arrived, tied = lax.optimization_barrier((onward, arrived, tied))
        states = tied.get("states", states)
        far = tied.get("far", {})
        groups.update(arrived)
        if not end:
            ring = onward[0]
            groups[dz + 1, 0] = onward
    stats = stage({key: list(range(len(chunks))) for key in groups}, last=True)

    levels = [1 << i for i in range(plan.V.bit_length() - 1)]
    if W == 4 and plan.V == 8:
        parts = [stats] + [move(stats, plan.vocab_xor(k)) for k in (3, 2, 1)]
        mine, other = call(
            functools.partial(split_kernel, plan, 4),
            [shape((4, plan.V // 2, part), jnp.float32)] * 2,
            parts,
            0,
            name="split",
        )
        arrived = [
            move(other, plan.perm(lambda v, w: (v ^ 4, w ^ 2))),
            move(mine, plan.vocab_xor(4)),
            move(other, plan.width_xor(2)),
        ]
        keep, passed = call(
            functools.partial(pair_kernel, plan),
            [shape((4 * blocks, part), jnp.float32)] * 2,
            (*arrived, mine),
            0,
            name="pair",
        )
        closed, order = [keep, move(passed, plan.width_xor(1))], (0, 2, 1, 3)
    else:
        rounds = [levels[i : i + 2] for i in range(0, len(levels), 2)]
        for i, level in enumerate(rounds):
            others = [level[0]] if len(level) == 1 else [level[0], level[1], level[0] | level[1]]
            parts = [stats] + [move(stats, plan.vocab_xor(k)) for k in others]
            if i + 1 < len(rounds):
                stats = call(
                    functools.partial(merge_kernel, len(parts)), shape(stats.shape, jnp.float32), parts, 0, name="merge"
                )
        closed = call(
            functools.partial(close_kernel, plan, len(parts)),
            [shape((2 * blocks, part), jnp.float32)] * W,
            parts,
            0,
            scratch=[pltpu.VMEM((2, plan.V, part), jnp.float32)],
            name="close",
        )
        closed = [closed[0]] + [move(closed[k], plan.width_xor(k)) for k in range(1, W)]
        order = tuple(range(W))
    return tuple(
        call(
            functools.partial(place_kernel, plan, len(closed), order),
            [shape(token_ids.shape, jnp.float32)] * 2,
            (seq_lengths, *closed),
            1,
            name="place",
        )
    )


def solution(mesh):
    in_specs = (P("vocab", "width"), P("width"), P("width", "vocab"), P("width"), P())
    out_specs = (P("width"), P("width"))
    return jax.shard_map(
        functools.partial(on_device, mesh), mesh=mesh, in_specs=in_specs, out_specs=out_specs, check_vma=False
    )
```

```python
import functools

import jax
import jax.numpy as jnp
from jax import lax
from jax.experimental import pallas as pl
from jax.experimental.pallas import tpu as pltpu
from jax.sharding import PartitionSpec as P

SEQ_LEN = 2048
EPS = 1e-06
LOW = -1e30
TILE = 256
EXTRA = 16
NEAR = 1024
AXES = ("vocab", "width")
VMEM = pl.BlockSpec(memory_space=pltpu.VMEM)
SMEM = pl.BlockSpec(memory_space=pltpu.SMEM)
HBM = pl.BlockSpec(memory_space=pltpu.HBM)


class Plan:
    def __init__(self, mesh, rows, columns):
        self.V, self.W = mesh.shape["vocab"], mesh.shape["width"]
        self.X = 1
        while 4 * self.X * self.X <= self.V:
            self.X *= 2
        self.Z = self.V // self.X
        self.rows = rows
        self.part = rows // self.W
        self.blocks = SEQ_LEN // rows
        self.columns = columns

    def perm(self, move):
        return [
            (v * self.W + w, t * self.W + u)
            for v in range(self.V)
            for w in range(self.W)
            for t, u in [move(v, w)]
        ]

    def width_xor(self, k):
        return self.perm(lambda v, w: (v, w ^ k))

    def vocab_xor(self, k):
        return self.perm(lambda v, w: (v ^ k, w))

    def z_ring(self):
        return self.perm(lambda v, w: ((v + self.X) % self.V, w))

    def x_ring(self):
        return self.perm(lambda v, w: (v - v % self.X + (v + 1) % self.X, w))


def quarter(plan, v, w):
    return lax.rem(w + v, plan.W)


def id_rows(plan, ids_ref, w, target):
    out = []
    for h in range(plan.blocks):
        q = quarter(plan, w * plan.blocks + h, target)
        start = pl.multiple_of((h * plan.W + q) * plan.part, plan.part)
        out.append(ids_ref[pl.ds(start, plan.part)].reshape(1, plan.part))
    return out


def send_kernel(plan, h_ref, gain_hbm, ids_hbm, *refs):
    outs, (gain_ref, ids_ref, sems) = refs[: plan.W], refs[plan.W :]
    v, w = lax.axis_index("vocab"), lax.axis_index("width")
    part = plan.part
    small = [
        pltpu.make_async_copy(gain_hbm, gain_ref, sems.at[0]),
        pltpu.make_async_copy(ids_hbm, ids_ref, sems.at[1]),
    ]
    for copy in small:
        copy.start()
    large = []
    for k in range(plan.W):
        start = pl.multiple_of(quarter(plan, v, w ^ k) * part, part)
        large.append(pltpu.make_async_copy(h_ref.at[pl.ds(start, part)], outs[k].at[pl.ds(0, part)], sems.at[2 + k]))
        large[-1].start()
    for copy in small:
        copy.wait()
    gain = gain_ref[...].reshape(1, gain_ref.shape[0])
    high = gain.astype(jnp.bfloat16).astype(jnp.float32)
    rest = gain - high
    middle = rest.astype(jnp.bfloat16).astype(jnp.float32)
    low = rest - middle
    width = gain.shape[1]
    for k in range(plan.W):
        rows = [high, middle, low]
        for line in id_rows(plan, ids_ref, w, w ^ k):
            upper = line // 256
            for piece in (upper, line - upper * 256):
                piece = piece.astype(jnp.float32)
                if part < width:
                    piece = jnp.concatenate([piece, jnp.zeros((1, width - part), jnp.float32)], axis=1)
                rows.append(piece[:, :width])
        rows.append(jnp.zeros((EXTRA - len(rows), width), jnp.float32))
        outs[k][part:, :] = jnp.concatenate(rows, axis=0).astype(jnp.bfloat16)
    for copy in large:
        copy.wait()


def norm_kernel(plan, depth, *refs):
    pieces, (out_ref, out_ids) = refs[: plan.W], refs[plan.W :]
    part, width = plan.part, depth // plan.W
    wide, gains = [], []
    for k in range(plan.W):
        wide.append(pieces[k][:part, :].astype(jnp.float32))
        extra = pieces[k][part:, :].astype(jnp.float32)
        gains.append((extra[0:1] + extra[1:2]) + extra[2:3])
        for h in range(plan.blocks):
            upper = extra[3 + 2 * h : 4 + 2 * h].astype(jnp.int32)
            under = extra[4 + 2 * h : 5 + 2 * h].astype(jnp.int32)
            row = k * plan.blocks + h
            out_ids[row : row + 1, :] = (upper * 256 + under)[:, :part]
    total = sum(jnp.sum(x * x, axis=1, keepdims=True) for x in wide)
    scale = lax.rsqrt(total / depth + EPS)
    for k in range(plan.W):
        normed = (wide[k] * scale * gains[k]).T
        out_ref[k * width : (k + 1) * width, :] = normed.astype(jnp.bfloat16)


def main_kernel(plan, jobs, sizes, bases, have, last, places, halves, where, offsets, seq_ref, ids_ref, *refs):
    refs = list(refs)
    take = lambda n: [refs.pop(0) for _ in range(n)]
    W, part = plan.W, plan.part
    groups = [take(n) for n in halves]
    held = take(max(where) + 1)
    chunks = [[held[i] for i in where[c * W : (c + 1) * W]] for c in range(len(sizes))]
    states = [take(1)[0] if h else None for h in have]
    outs = take(1 if last else len(jobs))
    buffers = take(2)
    v, w = lax.axis_index("vocab"), lax.axis_index("width")
    z, x = v // plan.X, lax.rem(v, plan.X)
    lane = (8, part)
    for g, mine in enumerate(jobs):
        dz, dx = places[g]
        source = lax.rem(z - dz + plan.Z, plan.Z) * plan.X + lax.rem(x - dx + plan.X, plan.X)
        s, h = source // plan.blocks, lax.rem(source, plan.blocks)
        first = h * plan.rows + quarter(plan, source, w) * part
        live = seq_ref[s] > first
        rank = (s ^ w) * plan.blocks + h

        def run(state):
            ids = jnp.broadcast_to(ids_ref[pl.ds(rank, 1), :], lane)
            ids = ids - lax.broadcasted_iota(jnp.int32, lane, 0) - v * plan.columns

            def right():
                held = [ref[...] for ref in groups[g]]
                return held[0] if len(held) == 1 else jnp.concatenate(held, axis=0)

            def dot(c, start, size):
                left = jnp.concatenate(
                    [ref[off + start : off + start + size, :] for ref, off in zip(chunks[c], offsets[c])], axis=1
                )
                return jnp.dot(left, right(), preferred_element_type=jnp.float32)

            def fold(state, buffer, size, base):
                m, e_sum, l_sum, target = state
                n = size // 8
                logits = buffer[:size, :].reshape((n,) + lane)
                top = jnp.maximum(m, jnp.max(logits, axis=0))
                scale = jnp.exp(m - top)
                terms = jnp.exp(logits - top[None])
                e_sum = e_sum * scale + jnp.sum(terms, axis=0)
                l_sum = l_sum * scale + jnp.sum(terms * logits, axis=0)
                there = ids - base
                for i in range(n):
                    target = jnp.where(there == 8 * i, logits[i], target)
                return top, e_sum, l_sum, target

            tiles = [(c, at, size) for c in mine for at, size in even(sizes[c], TILE)]
            buffers[0][: tiles[0][2], :] = dot(*tiles[0])
            for i, (c, at, size) in enumerate(tiles):
                if i + 1 < len(tiles):
                    buffers[1 - i % 2][: tiles[i + 1][2], :] = dot(*tiles[i + 1])
                state = fold(state, buffers[i % 2], size, bases[c] + at)
            return state

        def start_state():
            if have[g]:
                return tuple(states[g][i] for i in range(4))
            zero = jnp.zeros(lane, jnp.float32)
            return jnp.full(lane, LOW, jnp.float32), zero, zero, zero

        state = lax.cond(live, lambda: run(start_state()), start_state) if mine else start_state()
        if not last:
            for i in range(4):
                outs[g][i] = state[i]
            continue
        m, e_sum, l_sum, target = state
        top = jnp.max(m, axis=0, keepdims=True)
        scale = jnp.exp(m - top)
        lines = [top] + [jnp.sum(a, axis=0, keepdims=True) for a in (e_sum * scale, l_sum * scale, target)]
        for i, line in enumerate(lines):
            outs[0][i, pl.ds(source, 1), :] = line


def merge(parts):
    top = functools.reduce(jnp.maximum, [p[0] for p in parts])
    scales = [jnp.exp(p[0] - top) for p in parts]
    e_sum = sum(p[1] * c for p, c in zip(parts, scales))
    l_sum = sum(p[2] * c for p, c in zip(parts, scales))
    return top, e_sum, l_sum, sum(p[3] for p in parts)


def read(ref):
    return [ref[i] for i in range(4)]


def results(stats):
    top, e_sum, l_sum, target = stats
    logsum = top + jnp.log(e_sum)
    return target - logsum, logsum - l_sum / e_sum


def merge_kernel(count, *refs):
    for i, value in enumerate(merge([read(ref) for ref in refs[:count]])):
        refs[count][i] = value


def split_kernel(plan, count, *refs):
    mine, other = refs[count:]
    upper = lax.axis_index("width") // 2 == 1
    half = plan.V // 2
    for i, value in enumerate(merge([read(ref) for ref in refs[:count]])):
        mine[i] = jnp.where(upper, value[half:], value[:half])
        other[i] = jnp.where(upper, value[:half], value[half:])


def pair_kernel(plan, d_ref, b_ref, c_ref, a_ref, keep_ref, pass_ref):
    odd = lax.rem(lax.axis_index("width"), 2) == 1
    blocks = plan.blocks
    for n, (one, two) in enumerate(((a_ref, b_ref), (c_ref, d_ref))):
        for i, value in enumerate(results(merge([read(one), read(two)]))):
            rows = slice((2 * n + i) * blocks, (2 * n + i + 1) * blocks)
            keep_ref[rows, :] = jnp.where(odd, value[blocks:], value[:blocks])
            pass_ref[rows, :] = jnp.where(odd, value[:blocks], value[blocks:])


def close_kernel(plan, count, *refs):
    outs, held = refs[count:-1], refs[-1]
    w = lax.axis_index("width")
    for i, value in enumerate(results(merge([read(ref) for ref in refs[:count]]))):
        held[i] = value
    for k in range(plan.W):
        for h in range(plan.blocks):
            for i in range(2):
                row = i * plan.blocks + h
                outs[k][row : row + 1, :] = held[i, pl.ds((w ^ k) * plan.blocks + h, 1), :]


def place_kernel(plan, count, order, seq_ref, *refs):
    pieces, outs = refs[:count], refs[count:]
    w = lax.axis_index("width")
    length = seq_ref[w]
    column = lax.broadcasted_iota(jnp.int32, (1, plan.part), 1)
    sets = len(order) // count
    for n, k in enumerate(order):
        for h in range(plan.blocks):
            q = quarter(plan, w * plan.blocks + h, w ^ k)
            live = column + (h * plan.rows + q * plan.part) < length
            start = pl.multiple_of((h * plan.W + q) * plan.part, plan.part)
            for i in range(2):
                row = (2 * (n % sets) + i) * plan.blocks + h
                value = jnp.where(live, pieces[n // sets][row : row + 1, :], 0.0)
                outs[i][pl.ds(start, plan.part)] = value.reshape(plan.part)


def call(kernel, out_shape, args, smem, scratch=(), flops=0, name=None, far=0, limit=12):
    return pl.pallas_call(
        kernel,
        out_shape=out_shape,
        in_specs=[SMEM] * smem + [HBM] * far + [VMEM] * (len(args) - smem - far),
        out_specs=jax.tree.map(lambda _: VMEM, out_shape),
        scratch_shapes=list(scratch),
        compiler_params=pltpu.CompilerParams(vmem_limit_bytes=limit * 2**20),
        cost_estimate=pl.CostEstimate(flops=flops, bytes_accessed=0, transcendentals=0),
        name=name,
    )(*args)


def chunk_spans(columns, shares=(0.32, 0.701)):
    ends = [0] + [64 * round(columns * share / 64) for share in shares] + [columns]
    return [(a, b - a) for a, b in zip(ends, ends[1:])]


def even(size, most):
    step = -(-size // (16 * -(-size // most))) * 16
    return [(at, min(step, size - at)) for at in range(0, size, step)]


def tie(*values):
    return lax.optimization_barrier(values)


def on_device(mesh, hidden, norm_gain, head_weight, token_ids, seq_lengths):
    rows, width = hidden.shape
    columns = head_weight.shape[1]
    plan = Plan(mesh, rows, columns)
    W, part, blocks = plan.W, plan.part, plan.blocks
    depth = width * W
    shape = jax.ShapeDtypeStruct
    move = lambda value, perm: lax.ppermute(value, AXES, perm)

    sent = call(
        functools.partial(send_kernel, plan),
        [shape((part + EXTRA, width), jnp.bfloat16)] * W,
        [pltpu.with_memory_space_constraint(x, pltpu.HBM) for x in (hidden, norm_gain, token_ids)],
        0,
        scratch=[
            pltpu.VMEM((width,), jnp.float32),
            pltpu.VMEM(token_ids.shape, jnp.int32),
            pltpu.SemaphoreType.DMA((2 + W,)),
        ],
        name="send",
        far=3,
    )
    pieces = {k: move(sent[k], plan.width_xor(k)) for k in sorted(range(1, W), key=lambda k: (k != 1, -k))}
    pieces = [sent[0]] + [pieces[k] for k in range(1, W)]
    normed, all_ids = call(
        functools.partial(norm_kernel, plan, depth),
        [shape((depth, part), jnp.bfloat16), shape((W * blocks, part), jnp.int32)],
        pieces,
        0,
        name="norm",
    )

    spans = chunk_spans(columns)
    weight = head_weight.T
    bits = [1 << i for i in range(W.bit_length() - 1)]
    near = move(weight, plan.width_xor(1))

    def far_chunk(c, after):
        a, n = spans[c]
        held = {0: tie(weight[a : a + n], *after)[0]}
        for bit in reversed(bits[1:]):
            for k in list(held):
                held[k | bit] = move(held[k], plan.width_xor(bit))
        return held

    def near_chunk(c, held):
        start, size = spans[c]
        for at, count in even(size, NEAR):
            refs = {0: (weight, start + at), 1: (near, start + at)}
            for k in held:
                if k:
                    refs[k] = (held[k], at)
                    refs[k | 1] = (move(held[k][at : at + count], plan.width_xor(1)), 0)
            chunks.append([refs[k][0] for k in range(W)])
            firsts.append([refs[k][1] for k in range(W)])
            parts.append((start + at, count))

    states, groups, chunks, firsts, parts, done = {}, {}, [], [], [], {}

    def stage(wanted, last=False):
        jobs = {key: [c for c in mine if c not in done.get(key, [])] for key, mine in wanted.items()}
        done.update(wanted)
        keys = list(jobs)
        used = sorted({c for mine in jobs.values() for c in mine})
        have = [key in states for key in keys]
        sizes, bases = [parts[c][1] for c in used], [parts[c][0] for c in used]
        args = [seq_lengths, all_ids] + [part for key in keys if jobs[key] for part in groups[key]]
        halves = [len(groups[key]) if jobs[key] else 0 for key in keys]
        held = [chunks[c][k] for c in used for k in range(W)]
        offsets = [firsts[c] for c in used]
        unique = [held[i] for i in range(len(held)) if all(held[i] is not held[j] for j in range(i))]
        where = [next(j for j in range(len(unique)) if unique[j] is one) for one in held]
        args += unique
        args += [states[key] for key in keys if key in states]
        if last:
            out = [shape((4, plan.V, part), jnp.float32)]
        else:
            out = [shape((4, 8, part), jnp.float32)] * len(keys)
        work = sum(parts[c][1] for mine in jobs.values() for c in mine)
        got = call(
            functools.partial(
                main_kernel, plan, [[used.index(c) for c in jobs[key]] for key in keys], sizes, bases, have, last, keys,
                halves, where,
                offsets
            ),
            out,
            args,
            1,
            scratch=[pltpu.VMEM((TILE, part), jnp.float32)] * 2,
            flops=0,
            name="logits",
        )
        if last:
            return got[0]
        states.update(zip(keys, got))

    groups[0, 0] = [normed]
    ring, far = normed, {}
    fast = plan.X == 2 and plan.Z == 4
    for dz in range(plan.Z):
        end = dz == plan.Z - 1
        onward, arrived, tied = [], {}, {}
        if not end:
            onward = [move(ring, plan.z_ring())]
        if end and plan.X == 2:
            half = depth // 2
            arrived[dz, 1] = [
                move(ring[:half], plan.x_ring()),
                move(groups[dz - 1, 1][0][half:], plan.z_ring()),
            ]
        else:
            passed = ring
            for dx in range(1, plan.X):
                passed = move(passed, plan.x_ring())
                arrived[dz, dx] = [passed]
        if far:
            near_chunk(dz - 1, far)
        whole = len(chunks)
        if dz < len(spans):
            tied["far"] = far_chunk(dz, pieces[-1:])
        if fast and dz:
            stage({key: list(range(whole)) for key in groups})
            tied["states"] = states
        if dz == len(spans) - 1:
            held, states = lax.optimization_barrier((tied.pop("far"), states))
            near_chunk(dz, held)
            tied["last"] = chunks[whole:]
            if fast:
                tied["states"] = states
        onward, arrived, tied = lax.optimization_barrier((onward, arrived, tied))
        states = tied.get("states", states)
        far = tied.get("far", {})
        chunks[whole:] = tied.get("last", [])
        groups.update(arrived)
        if not end:
            ring = onward[0]
            groups[dz + 1, 0] = onward
    stats = stage({key: list(range(len(chunks))) for key in groups}, last=True)

    levels = [1 << i for i in range(plan.V.bit_length() - 1)]
    if W == 4 and plan.V == 8:
        parts = [stats] + [move(stats, plan.vocab_xor(k)) for k in (3, 2, 1)]
        mine, other = call(
            functools.partial(split_kernel, plan, 4),
            [shape((4, plan.V // 2, part), jnp.float32)] * 2,
            parts,
            0,
            name="split",
        )
        arrived = [
            move(other, plan.perm(lambda v, w: (v ^ 4, w ^ 2))),
            move(mine, plan.vocab_xor(4)),
            move(other, plan.width_xor(2)),
        ]
        keep, passed = call(
            functools.partial(pair_kernel, plan),
            [shape((4 * blocks, part), jnp.float32)] * 2,
            (*arrived, mine),
            0,
            name="pair",
        )
        closed, order = [keep, move(passed, plan.width_xor(1))], (0, 2, 1, 3)
    else:
        rounds = [levels[i : i + 2] for i in range(0, len(levels), 2)]
        for i, level in enumerate(rounds):
            others = [level[0]] if len(level) == 1 else [level[0], level[1], level[0] | level[1]]
            parts = [stats] + [move(stats, plan.vocab_xor(k)) for k in others]
            if i + 1 < len(rounds):
                stats = call(
                    functools.partial(merge_kernel, len(parts)), shape(stats.shape, jnp.float32), parts, 0, name="merge"
                )
        closed = call(
            functools.partial(close_kernel, plan, len(parts)),
            [shape((2 * blocks, part), jnp.float32)] * W,
            parts,
            0,
            scratch=[pltpu.VMEM((2, plan.V, part), jnp.float32)],
            name="close",
        )
        closed = [closed[0]] + [move(closed[k], plan.width_xor(k)) for k in range(1, W)]
        order = tuple(range(W))
    return tuple(
        call(
            functools.partial(place_kernel, plan, len(closed), order),
            [shape(token_ids.shape, jnp.float32)] * 2,
            (seq_lengths, *closed),
            1,
            name="place",
        )
    )


def solution(mesh):
    in_specs = (P("vocab", "width"), P("width"), P("width", "vocab"), P("width"), P())
    out_specs = (P("width"), P("width"))
    return jax.shard_map(
        functools.partial(on_device, mesh), mesh=mesh, in_specs=in_specs, out_specs=out_specs, check_vma=False
    )
```

```python
import functools

import jax
import jax.numpy as jnp
from jax import lax
from jax.experimental import pallas as pl
from jax.experimental.pallas import tpu as pltpu
from jax.sharding import PartitionSpec as P

SEQ_LEN = 2048
EPS = 1e-06
LOW = -1e30
TILE = 256
EXTRA = 16
NEAR = 1024
AXES = ("vocab", "width")
VMEM = pl.BlockSpec(memory_space=pltpu.VMEM)
SMEM = pl.BlockSpec(memory_space=pltpu.SMEM)
HBM = pl.BlockSpec(memory_space=pltpu.HBM)


class Plan:
    def __init__(self, mesh, rows, columns):
        self.V, self.W = mesh.shape["vocab"], mesh.shape["width"]
        self.X = 1
        while 4 * self.X * self.X <= self.V:
            self.X *= 2
        self.Z = self.V // self.X
        self.rows = rows
        self.part = rows // self.W
        self.blocks = SEQ_LEN // rows
        self.columns = columns

    def perm(self, move):
        return [
            (v * self.W + w, t * self.W + u)
            for v in range(self.V)
            for w in range(self.W)
            for t, u in [move(v, w)]
        ]

    def width_xor(self, k):
        return self.perm(lambda v, w: (v, w ^ k))

    def vocab_xor(self, k):
        return self.perm(lambda v, w: (v ^ k, w))

    def z_ring(self):
        return self.perm(lambda v, w: ((v + self.X) % self.V, w))

    def x_ring(self):
        return self.perm(lambda v, w: (v - v % self.X + (v + 1) % self.X, w))


def quarter(plan, v, w):
    return lax.rem(w + v, plan.W)


def id_rows(plan, ids_ref, w, target):
    out = []
    for h in range(plan.blocks):
        q = quarter(plan, w * plan.blocks + h, target)
        start = pl.multiple_of((h * plan.W + q) * plan.part, plan.part)
        out.append(ids_ref[pl.ds(start, plan.part)].reshape(1, plan.part))
    return out


def send_kernel(plan, h_ref, gain_hbm, ids_hbm, *refs):
    outs, (gain_ref, ids_ref, sems) = refs[: plan.W], refs[plan.W :]
    v, w = lax.axis_index("vocab"), lax.axis_index("width")
    part = plan.part
    small = [
        pltpu.make_async_copy(gain_hbm, gain_ref, sems.at[0]),
        pltpu.make_async_copy(ids_hbm, ids_ref, sems.at[1]),
    ]
    for copy in small:
        copy.start()
    large = []
    for k in range(plan.W):
        start = pl.multiple_of(quarter(plan, v, w ^ k) * part, part)
        large.append(pltpu.make_async_copy(h_ref.at[pl.ds(start, part)], outs[k].at[pl.ds(0, part)], sems.at[2 + k]))
        large[-1].start()
    for copy in small:
        copy.wait()
    gain = gain_ref[...].reshape(1, gain_ref.shape[0])
    high = gain.astype(jnp.bfloat16).astype(jnp.float32)
    rest = gain - high
    middle = rest.astype(jnp.bfloat16).astype(jnp.float32)
    low = rest - middle
    width = gain.shape[1]
    for k in range(plan.W):
        rows = [high, middle, low]
        for line in id_rows(plan, ids_ref, w, w ^ k):
            upper = line // 256
            for piece in (upper, line - upper * 256):
                piece = piece.astype(jnp.float32)
                if part < width:
                    piece = jnp.concatenate([piece, jnp.zeros((1, width - part), jnp.float32)], axis=1)
                rows.append(piece[:, :width])
        rows.append(jnp.zeros((EXTRA - len(rows), width), jnp.float32))
        outs[k][part:, :] = jnp.concatenate(rows, axis=0).astype(jnp.bfloat16)
    for copy in large:
        copy.wait()


def norm_kernel(plan, depth, *refs):
    pieces, (out_ref, out_ids) = refs[: plan.W], refs[plan.W :]
    part, width = plan.part, depth // plan.W
    wide, gains = [], []
    for k in range(plan.W):
        wide.append(pieces[k][:part, :].astype(jnp.float32))
        extra = pieces[k][part:, :].astype(jnp.float32)
        gains.append((extra[0:1] + extra[1:2]) + extra[2:3])
        for h in range(plan.blocks):
            upper = extra[3 + 2 * h : 4 + 2 * h].astype(jnp.int32)
            under = extra[4 + 2 * h : 5 + 2 * h].astype(jnp.int32)
            row = k * plan.blocks + h
            out_ids[row : row + 1, :] = (upper * 256 + under)[:, :part]
    total = sum(jnp.sum(x * x, axis=1, keepdims=True) for x in wide)
    scale = lax.rsqrt(total / depth + EPS)
    for k in range(plan.W):
        normed = (wide[k] * scale * gains[k]).T
        out_ref[k * width : (k + 1) * width, :] = normed.astype(jnp.bfloat16)


def main_kernel(plan, jobs, sizes, bases, have, last, places, halves, where, offsets, seq_ref, ids_ref, *refs):
    refs = list(refs)
    take = lambda n: [refs.pop(0) for _ in range(n)]
    W, part = plan.W, plan.part
    groups = [take(n) for n in halves]
    held = take(max(where) + 1)
    chunks = [[held[i] for i in where[c * W : (c + 1) * W]] for c in range(len(sizes))]
    states = [take(1)[0] if h else None for h in have]
    outs = take(1 if last else len(jobs))
    buffers = take(2)
    v, w = lax.axis_index("vocab"), lax.axis_index("width")
    z, x = v // plan.X, lax.rem(v, plan.X)
    lane = (8, part)
    for g, mine in enumerate(jobs):
        dz, dx = places[g]
        source = lax.rem(z - dz + plan.Z, plan.Z) * plan.X + lax.rem(x - dx + plan.X, plan.X)
        s, h = source // plan.blocks, lax.rem(source, plan.blocks)
        first = h * plan.rows + quarter(plan, source, w) * part
        live = seq_ref[s] > first
        rank = (s ^ w) * plan.blocks + h

        def run(state):
            ids = jnp.broadcast_to(ids_ref[pl.ds(rank, 1), :], lane)
            ids = ids - lax.broadcasted_iota(jnp.int32, lane, 0) - v * plan.columns

            def right():
                held = [ref[...] for ref in groups[g]]
                return held[0] if len(held) == 1 else jnp.concatenate(held, axis=0)

            def dot(c, start, size):
                left = jnp.concatenate(
                    [ref[off + start : off + start + size, :] for ref, off in zip(chunks[c], offsets[c])], axis=1
                )
                return jnp.dot(left, right(), preferred_element_type=jnp.float32)

            def fold(state, buffer, size, base):
                m, e_sum, l_sum, target = state
                n = size // 8
                logits = buffer[:size, :].reshape((n,) + lane)
                top = jnp.maximum(m, jnp.max(logits, axis=0))
                scale = jnp.exp(m - top)
                terms = jnp.exp(logits - top[None])
                e_sum = e_sum * scale + jnp.sum(terms, axis=0)
                l_sum = l_sum * scale + jnp.sum(terms * logits, axis=0)
                there = ids - base
                for i in range(n):
                    target = jnp.where(there == 8 * i, logits[i], target)
                return top, e_sum, l_sum, target

            tiles = [(c, at, size) for c in mine for at, size in even(sizes[c], TILE)]
            buffers[0][: tiles[0][2], :] = dot(*tiles[0])
            for i, (c, at, size) in enumerate(tiles):
                if i + 1 < len(tiles):
                    buffers[1 - i % 2][: tiles[i + 1][2], :] = dot(*tiles[i + 1])
                state = fold(state, buffers[i % 2], size, bases[c] + at)
            return state

        def start_state():
            if have[g]:
                return tuple(states[g][i] for i in range(4))
            zero = jnp.zeros(lane, jnp.float32)
            return jnp.full(lane, LOW, jnp.float32), zero, zero, zero

        state = lax.cond(live, lambda: run(start_state()), start_state) if mine else start_state()
        if not last:
            for i in range(4):
                outs[g][i] = state[i]
            continue
        m, e_sum, l_sum, target = state
        top = jnp.max(m, axis=0, keepdims=True)
        scale = jnp.exp(m - top)
        lines = [top] + [jnp.sum(a, axis=0, keepdims=True) for a in (e_sum * scale, l_sum * scale, target)]
        for i, line in enumerate(lines):
            outs[0][i, pl.ds(source, 1), :] = line


def merge(parts):
    top = functools.reduce(jnp.maximum, [p[0] for p in parts])
    scales = [jnp.exp(p[0] - top) for p in parts]
    e_sum = sum(p[1] * c for p, c in zip(parts, scales))
    l_sum = sum(p[2] * c for p, c in zip(parts, scales))
    return top, e_sum, l_sum, sum(p[3] for p in parts)


def read(ref):
    return [ref[i] for i in range(4)]


def results(stats):
    top, e_sum, l_sum, target = stats
    logsum = top + jnp.log(e_sum)
    return target - logsum, logsum - l_sum / e_sum


def merge_kernel(count, *refs):
    for i, value in enumerate(merge([read(ref) for ref in refs[:count]])):
        refs[count][i] = value


def split_kernel(plan, count, *refs):
    mine, other = refs[count:]
    upper = lax.axis_index("width") // 2 == 1
    half = plan.V // 2
    for i, value in enumerate(merge([read(ref) for ref in refs[:count]])):
        mine[i] = jnp.where(upper, value[half:], value[:half])
        other[i] = jnp.where(upper, value[:half], value[half:])


def pair_kernel(plan, d_ref, b_ref, c_ref, a_ref, keep_ref, pass_ref):
    odd = lax.rem(lax.axis_index("width"), 2) == 1
    blocks = plan.blocks
    for n, (one, two) in enumerate(((a_ref, b_ref), (c_ref, d_ref))):
        for i, value in enumerate(results(merge([read(one), read(two)]))):
            rows = slice((2 * n + i) * blocks, (2 * n + i + 1) * blocks)
            keep_ref[rows, :] = jnp.where(odd, value[blocks:], value[:blocks])
            pass_ref[rows, :] = jnp.where(odd, value[:blocks], value[blocks:])


def close_kernel(plan, count, *refs):
    outs, held = refs[count:-1], refs[-1]
    w = lax.axis_index("width")
    for i, value in enumerate(results(merge([read(ref) for ref in refs[:count]]))):
        held[i] = value
    for k in range(plan.W):
        for h in range(plan.blocks):
            for i in range(2):
                row = i * plan.blocks + h
                outs[k][row : row + 1, :] = held[i, pl.ds((w ^ k) * plan.blocks + h, 1), :]


def place_kernel(plan, count, order, seq_ref, *refs):
    pieces, outs = refs[:count], refs[count:]
    w = lax.axis_index("width")
    length = seq_ref[w]
    column = lax.broadcasted_iota(jnp.int32, (1, plan.part), 1)
    sets = len(order) // count
    for n, k in enumerate(order):
        for h in range(plan.blocks):
            q = quarter(plan, w * plan.blocks + h, w ^ k)
            live = column + (h * plan.rows + q * plan.part) < length
            start = pl.multiple_of((h * plan.W + q) * plan.part, plan.part)
            for i in range(2):
                row = (2 * (n % sets) + i) * plan.blocks + h
                value = jnp.where(live, pieces[n // sets][row : row + 1, :], 0.0)
                outs[i][pl.ds(start, plan.part)] = value.reshape(plan.part)


def call(kernel, out_shape, args, smem, scratch=(), flops=0, name=None, far=0, limit=12):
    return pl.pallas_call(
        kernel,
        out_shape=out_shape,
        in_specs=[SMEM] * smem + [HBM] * far + [VMEM] * (len(args) - smem - far),
        out_specs=jax.tree.map(lambda _: VMEM, out_shape),
        scratch_shapes=list(scratch),
        compiler_params=pltpu.CompilerParams(vmem_limit_bytes=limit * 2**20),
        cost_estimate=pl.CostEstimate(flops=flops, bytes_accessed=0, transcendentals=0),
        name=name,
    )(*args)


def chunk_spans(columns, shares=(0.32, 0.685)):
    ends = [0] + [64 * round(columns * share / 64) for share in shares] + [columns]
    return [(a, b - a) for a, b in zip(ends, ends[1:])]


def even(size, most):
    step = -(-size // (16 * -(-size // most))) * 16
    return [(at, min(step, size - at)) for at in range(0, size, step)]


def tie(*values):
    return lax.optimization_barrier(values)


def on_device(mesh, hidden, norm_gain, head_weight, token_ids, seq_lengths):
    rows, width = hidden.shape
    columns = head_weight.shape[1]
    plan = Plan(mesh, rows, columns)
    W, part, blocks = plan.W, plan.part, plan.blocks
    depth = width * W
    shape = jax.ShapeDtypeStruct
    move = lambda value, perm: lax.ppermute(value, AXES, perm)

    sent = call(
        functools.partial(send_kernel, plan),
        [shape((part + EXTRA, width), jnp.bfloat16)] * W,
        [pltpu.with_memory_space_constraint(x, pltpu.HBM) for x in (hidden, norm_gain, token_ids)],
        0,
        scratch=[
            pltpu.VMEM((width,), jnp.float32),
            pltpu.VMEM(token_ids.shape, jnp.int32),
            pltpu.SemaphoreType.DMA((2 + W,)),
        ],
        name="send",
        far=3,
    )
    pieces = {k: move(sent[k], plan.width_xor(k)) for k in sorted(range(1, W), key=lambda k: (k != 1, -k))}
    pieces = [sent[0]] + [pieces[k] for k in range(1, W)]
    normed, all_ids = call(
        functools.partial(norm_kernel, plan, depth),
        [shape((depth, part), jnp.bfloat16), shape((W * blocks, part), jnp.int32)],
        pieces,
        0,
        name="norm",
    )

    spans = chunk_spans(columns)
    weight = head_weight.T
    bits = [1 << i for i in range(W.bit_length() - 1)]
    near = move(weight, plan.width_xor(1))

    def far_chunk(c, after):
        a, n = spans[c]
        held = {0: tie(weight[a : a + n], *after)[0]}
        for bit in reversed(bits[1:]):
            for k in list(held):
                held[k | bit] = move(held[k], plan.width_xor(bit))
        return held

    def near_chunk(c, held):
        start, size = spans[c]
        for at, count in even(size, NEAR):
            refs = {0: (weight, start + at), 1: (near, start + at)}
            for k in held:
                if k:
                    refs[k] = (held[k], at)
                    refs[k | 1] = (move(held[k][at : at + count], plan.width_xor(1)), 0)
            chunks.append([refs[k][0] for k in range(W)])
            firsts.append([refs[k][1] for k in range(W)])
            parts.append((start + at, count))

    states, groups, chunks, firsts, parts, done = {}, {}, [], [], [], {}

    def stage(wanted, last=False):
        jobs = {key: [c for c in mine if c not in done.get(key, [])] for key, mine in wanted.items()}
        done.update(wanted)
        keys = list(jobs)
        used = sorted({c for mine in jobs.values() for c in mine})
        have = [key in states for key in keys]
        sizes, bases = [parts[c][1] for c in used], [parts[c][0] for c in used]
        args = [seq_lengths, all_ids] + [part for key in keys if jobs[key] for part in groups[key]]
        halves = [len(groups[key]) if jobs[key] else 0 for key in keys]
        held = [chunks[c][k] for c in used for k in range(W)]
        offsets = [firsts[c] for c in used]
        unique = [held[i] for i in range(len(held)) if all(held[i] is not held[j] for j in range(i))]
        where = [next(j for j in range(len(unique)) if unique[j] is one) for one in held]
        args += unique
        args += [states[key] for key in keys if key in states]
        if last:
            out = [shape((4, plan.V, part), jnp.float32)]
        else:
            out = [shape((4, 8, part), jnp.float32)] * len(keys)
        work = sum(parts[c][1] for mine in jobs.values() for c in mine)
        got = call(
            functools.partial(
                main_kernel, plan, [[used.index(c) for c in jobs[key]] for key in keys], sizes, bases, have, last, keys,
                halves, where,
                offsets
            ),
            out,
            args,
            1,
            scratch=[pltpu.VMEM((TILE, part), jnp.float32)] * 2,
            flops=0,
            name="logits",
        )
        if last:
            return got[0]
        states.update(zip(keys, got))

    groups[0, 0] = [normed]
    ring, far = normed, {}
    fast = plan.X == 2 and plan.Z == 4
    for dz in range(plan.Z):
        end = dz == plan.Z - 1
        onward, arrived, tied = [], {}, {}
        if not end:
            onward = [move(ring, plan.z_ring())]
        if end and plan.X == 2:
            half = depth // 2
            arrived[dz, 1] = [
                move(ring[:half], plan.x_ring()),
                move(groups[dz - 1, 1][0][half:], plan.z_ring()),
            ]
        else:
            passed = ring
            for dx in range(1, plan.X):
                passed = move(passed, plan.x_ring())
                arrived[dz, dx] = [passed]
        if far:
            near_chunk(dz - 1, far)
        whole = len(chunks)
        if dz == 0:
            tied["near"] = near
        if dz < len(spans):
            tied["far"] = far_chunk(dz, pieces[-1:])
        if fast and dz:
            stage({key: list(range(whole)) for key in groups})
            tied["states"] = states
        if dz == len(spans) - 1:
            held, states = lax.optimization_barrier((tied.pop("far"), states))
            near_chunk(dz, held)
            tied["last"] = chunks[whole:]
            if fast:
                tied["states"] = states
        onward, arrived, tied = lax.optimization_barrier((onward, arrived, tied))
        states = tied.get("states", states)
        far = tied.get("far", {})
        near = tied.get("near", near)
        chunks[whole:] = tied.get("last", [])
        groups.update(arrived)
        if not end:
            ring = onward[0]
            groups[dz + 1, 0] = onward
    stats = stage({key: list(range(len(chunks))) for key in groups}, last=True)

    levels = [1 << i for i in range(plan.V.bit_length() - 1)]
    if W == 4 and plan.V == 8:
        parts = [stats] + [move(stats, plan.vocab_xor(k)) for k in (3, 2, 1)]
        mine, other = call(
            functools.partial(split_kernel, plan, 4),
            [shape((4, plan.V // 2, part), jnp.float32)] * 2,
            parts,
            0,
            name="split",
        )
        arrived = [
            move(other, plan.perm(lambda v, w: (v ^ 4, w ^ 2))),
            move(mine, plan.vocab_xor(4)),
            move(other, plan.width_xor(2)),
        ]
        keep, passed = call(
            functools.partial(pair_kernel, plan),
            [shape((4 * blocks, part), jnp.float32)] * 2,
            (*arrived, mine),
            0,
            name="pair",
        )
        closed, order = [keep, move(passed, plan.width_xor(1))], (0, 2, 1, 3)
    else:
        rounds = [levels[i : i + 2] for i in range(0, len(levels), 2)]
        for i, level in enumerate(rounds):
            others = [level[0]] if len(level) == 1 else [level[0], level[1], level[0] | level[1]]
            parts = [stats] + [move(stats, plan.vocab_xor(k)) for k in others]
            if i + 1 < len(rounds):
                stats = call(
                    functools.partial(merge_kernel, len(parts)), shape(stats.shape, jnp.float32), parts, 0, name="merge"
                )
        closed = call(
            functools.partial(close_kernel, plan, len(parts)),
            [shape((2 * blocks, part), jnp.float32)] * W,
            parts,
            0,
            scratch=[pltpu.VMEM((2, plan.V, part), jnp.float32)],
            name="close",
        )
        closed = [closed[0]] + [move(closed[k], plan.width_xor(k)) for k in range(1, W)]
        order = tuple(range(W))
    return tuple(
        call(
            functools.partial(place_kernel, plan, len(closed), order),
            [shape(token_ids.shape, jnp.float32)] * 2,
            (seq_lengths, *closed),
            1,
            name="place",
        )
    )


def solution(mesh):
    in_specs = (P("vocab", "width"), P("width"), P("width", "vocab"), P("width"), P())
    out_specs = (P("width"), P("width"))
    return jax.shard_map(
        functools.partial(on_device, mesh), mesh=mesh, in_specs=in_specs, out_specs=out_specs, check_vma=False
    )
```

```python
import functools

import jax
import jax.numpy as jnp
from jax import lax
from jax.experimental import pallas as pl
from jax.experimental.pallas import tpu as pltpu
from jax.sharding import PartitionSpec as P

SEQ_LEN = 2048
EPS = 1e-06
LOW = -1e30
TILE = 256
EXTRA = 16
NEAR = 1024
AXES = ("vocab", "width")
VMEM = pl.BlockSpec(memory_space=pltpu.VMEM)
SMEM = pl.BlockSpec(memory_space=pltpu.SMEM)
HBM = pl.BlockSpec(memory_space=pltpu.HBM)


class Plan:
    def __init__(self, mesh, rows, columns):
        self.V, self.W = mesh.shape["vocab"], mesh.shape["width"]
        self.X = 1
        while 4 * self.X * self.X <= self.V:
            self.X *= 2
        self.Z = self.V // self.X
        self.rows = rows
        self.part = rows // self.W
        self.blocks = SEQ_LEN // rows
        self.columns = columns

    def perm(self, move):
        return [
            (v * self.W + w, t * self.W + u)
            for v in range(self.V)
            for w in range(self.W)
            for t, u in [move(v, w)]
        ]

    def width_xor(self, k):
        return self.perm(lambda v, w: (v, w ^ k))

    def vocab_xor(self, k):
        return self.perm(lambda v, w: (v ^ k, w))

    def z_ring(self):
        return self.perm(lambda v, w: ((v + self.X) % self.V, w))

    def x_ring(self):
        return self.perm(lambda v, w: (v - v % self.X + (v + 1) % self.X, w))


def quarter(plan, v, w):
    return lax.rem(w + v, plan.W)


def id_rows(plan, ids_ref, w, target):
    out = []
    for h in range(plan.blocks):
        q = quarter(plan, w * plan.blocks + h, target)
        start = pl.multiple_of((h * plan.W + q) * plan.part, plan.part)
        out.append(ids_ref[pl.ds(start, plan.part)].reshape(1, plan.part))
    return out


def send_kernel(plan, h_ref, gain_hbm, ids_hbm, *refs):
    outs, (gain_ref, ids_ref, sems) = refs[: plan.W], refs[plan.W :]
    v, w = lax.axis_index("vocab"), lax.axis_index("width")
    part = plan.part
    small = [
        pltpu.make_async_copy(gain_hbm, gain_ref, sems.at[0]),
        pltpu.make_async_copy(ids_hbm, ids_ref, sems.at[1]),
    ]
    for copy in small:
        copy.start()
    large = []
    for k in range(plan.W):
        start = pl.multiple_of(quarter(plan, v, w ^ k) * part, part)
        large.append(pltpu.make_async_copy(h_ref.at[pl.ds(start, part)], outs[k].at[pl.ds(0, part)], sems.at[2 + k]))
        large[-1].start()
    for copy in small:
        copy.wait()
    gain = gain_ref[...].reshape(1, gain_ref.shape[0])
    high = gain.astype(jnp.bfloat16).astype(jnp.float32)
    rest = gain - high
    middle = rest.astype(jnp.bfloat16).astype(jnp.float32)
    low = rest - middle
    width = gain.shape[1]
    for k in range(plan.W):
        rows = [high, middle, low]
        for line in id_rows(plan, ids_ref, w, w ^ k):
            upper = line // 256
            for piece in (upper, line - upper * 256):
                piece = piece.astype(jnp.float32)
                if part < width:
                    piece = jnp.concatenate([piece, jnp.zeros((1, width - part), jnp.float32)], axis=1)
                rows.append(piece[:, :width])
        rows.append(jnp.zeros((EXTRA - len(rows), width), jnp.float32))
        outs[k][part:, :] = jnp.concatenate(rows, axis=0).astype(jnp.bfloat16)
    for copy in large:
        copy.wait()


def norm_kernel(plan, depth, *refs):
    pieces, (out_ref, out_ids) = refs[: plan.W], refs[plan.W :]
    part, width = plan.part, depth // plan.W
    wide, gains = [], []
    for k in range(plan.W):
        wide.append(pieces[k][:part, :].astype(jnp.float32))
        extra = pieces[k][part:, :].astype(jnp.float32)
        gains.append((extra[0:1] + extra[1:2]) + extra[2:3])
        for h in range(plan.blocks):
            upper = extra[3 + 2 * h : 4 + 2 * h].astype(jnp.int32)
            under = extra[4 + 2 * h : 5 + 2 * h].astype(jnp.int32)
            row = k * plan.blocks + h
            out_ids[row : row + 1, :] = (upper * 256 + under)[:, :part]
    total = sum(jnp.sum(x * x, axis=1, keepdims=True) for x in wide)
    scale = lax.rsqrt(total / depth + EPS)
    for k in range(plan.W):
        normed = (wide[k] * scale * gains[k]).T
        out_ref[k * width : (k + 1) * width, :] = normed.astype(jnp.bfloat16)


def main_kernel(plan, jobs, sizes, bases, have, last, places, halves, where, offsets, seq_ref, ids_ref, *refs):
    refs = list(refs)
    take = lambda n: [refs.pop(0) for _ in range(n)]
    W, part = plan.W, plan.part
    groups = [take(n) for n in halves]
    held = take(max(where) + 1)
    chunks = [[held[i] for i in where[c * W : (c + 1) * W]] for c in range(len(sizes))]
    states = [take(1)[0] if h else None for h in have]
    outs = take(1 if last else len(jobs))
    buffers = take(2)
    v, w = lax.axis_index("vocab"), lax.axis_index("width")
    z, x = v // plan.X, lax.rem(v, plan.X)
    lane = (8, part)
    for g, mine in enumerate(jobs):
        dz, dx = places[g]
        source = lax.rem(z - dz + plan.Z, plan.Z) * plan.X + lax.rem(x - dx + plan.X, plan.X)
        s, h = source // plan.blocks, lax.rem(source, plan.blocks)
        first = h * plan.rows + quarter(plan, source, w) * part
        live = seq_ref[s] > first
        rank = (s ^ w) * plan.blocks + h

        def run(state):
            ids = jnp.broadcast_to(ids_ref[pl.ds(rank, 1), :], lane)
            ids = ids - lax.broadcasted_iota(jnp.int32, lane, 0) - v * plan.columns

            def right():
                held = [ref[...] for ref in groups[g]]
                return held[0] if len(held) == 1 else jnp.concatenate(held, axis=0)

            def dot(c, start, size):
                left = jnp.concatenate(
                    [ref[off + start : off + start + size, :] for ref, off in zip(chunks[c], offsets[c])], axis=1
                )
                return jnp.dot(left, right(), preferred_element_type=jnp.float32)

            def fold(state, buffer, size, base):
                m, e_sum, l_sum, target = state
                n = size // 8
                logits = buffer[:size, :].reshape((n,) + lane)
                top = jnp.maximum(m, jnp.max(logits, axis=0))
                scale = jnp.exp(m - top)
                terms = jnp.exp(logits - top[None])
                e_sum = e_sum * scale + jnp.sum(terms, axis=0)
                l_sum = l_sum * scale + jnp.sum(terms * logits, axis=0)
                there = ids - base
                for i in range(n):
                    target = jnp.where(there == 8 * i, logits[i], target)
                return top, e_sum, l_sum, target

            tiles = [(c, at, size) for c in mine for at, size in even(sizes[c], TILE)]
            buffers[0][: tiles[0][2], :] = dot(*tiles[0])
            for i, (c, at, size) in enumerate(tiles):
                if i + 1 < len(tiles):
                    buffers[1 - i % 2][: tiles[i + 1][2], :] = dot(*tiles[i + 1])
                state = fold(state, buffers[i % 2], size, bases[c] + at)
            return state

        def start_state():
            if have[g]:
                return tuple(states[g][i] for i in range(4))
            zero = jnp.zeros(lane, jnp.float32)
            return jnp.full(lane, LOW, jnp.float32), zero, zero, zero

        state = lax.cond(live, lambda: run(start_state()), start_state) if mine else start_state()
        if not last:
            for i in range(4):
                outs[g][i] = state[i]
            continue
        m, e_sum, l_sum, target = state
        top = jnp.max(m, axis=0, keepdims=True)
        scale = jnp.exp(m - top)
        lines = [top] + [jnp.sum(a, axis=0, keepdims=True) for a in (e_sum * scale, l_sum * scale, target)]
        for i, line in enumerate(lines):
            outs[0][i, pl.ds(source, 1), :] = line


def merge(parts):
    top = functools.reduce(jnp.maximum, [p[0] for p in parts])
    scales = [jnp.exp(p[0] - top) for p in parts]
    e_sum = sum(p[1] * c for p, c in zip(parts, scales))
    l_sum = sum(p[2] * c for p, c in zip(parts, scales))
    return top, e_sum, l_sum, sum(p[3] for p in parts)


def read(ref):
    return [ref[i] for i in range(4)]


def results(stats):
    top, e_sum, l_sum, target = stats
    logsum = top + jnp.log(e_sum)
    return target - logsum, logsum - l_sum / e_sum


def merge_kernel(count, *refs):
    for i, value in enumerate(merge([read(ref) for ref in refs[:count]])):
        refs[count][i] = value


def split_kernel(plan, count, *refs):
    mine, other = refs[count:]
    upper = lax.axis_index("width") // 2 == 1
    half = plan.V // 2
    for i, value in enumerate(merge([read(ref) for ref in refs[:count]])):
        mine[i] = jnp.where(upper, value[half:], value[:half])
        other[i] = jnp.where(upper, value[:half], value[half:])


def pair_kernel(plan, d_ref, b_ref, c_ref, a_ref, keep_ref, pass_ref):
    odd = lax.rem(lax.axis_index("width"), 2) == 1
    blocks = plan.blocks
    for n, (one, two) in enumerate(((a_ref, b_ref), (c_ref, d_ref))):
        for i, value in enumerate(results(merge([read(one), read(two)]))):
            rows = slice((2 * n + i) * blocks, (2 * n + i + 1) * blocks)
            keep_ref[rows, :] = jnp.where(odd, value[blocks:], value[:blocks])
            pass_ref[rows, :] = jnp.where(odd, value[:blocks], value[blocks:])


def close_kernel(plan, count, *refs):
    outs, held = refs[count:-1], refs[-1]
    w = lax.axis_index("width")
    for i, value in enumerate(results(merge([read(ref) for ref in refs[:count]]))):
        held[i] = value
    for k in range(plan.W):
        for h in range(plan.blocks):
            for i in range(2):
                row = i * plan.blocks + h
                outs[k][row : row + 1, :] = held[i, pl.ds((w ^ k) * plan.blocks + h, 1), :]


def place_kernel(plan, count, order, seq_ref, *refs):
    pieces, outs = refs[:count], refs[count:]
    w = lax.axis_index("width")
    length = seq_ref[w]
    column = lax.broadcasted_iota(jnp.int32, (1, plan.part), 1)
    sets = len(order) // count
    for n, k in enumerate(order):
        for h in range(plan.blocks):
            q = quarter(plan, w * plan.blocks + h, w ^ k)
            live = column + (h * plan.rows + q * plan.part) < length
            start = pl.multiple_of((h * plan.W + q) * plan.part, plan.part)
            for i in range(2):
                row = (2 * (n % sets) + i) * plan.blocks + h
                value = jnp.where(live, pieces[n // sets][row : row + 1, :], 0.0)
                outs[i][pl.ds(start, plan.part)] = value.reshape(plan.part)


def call(kernel, out_shape, args, smem, scratch=(), flops=0, name=None, far=0, limit=12):
    return pl.pallas_call(
        kernel,
        out_shape=out_shape,
        in_specs=[SMEM] * smem + [HBM] * far + [VMEM] * (len(args) - smem - far),
        out_specs=jax.tree.map(lambda _: VMEM, out_shape),
        scratch_shapes=list(scratch),
        compiler_params=pltpu.CompilerParams(vmem_limit_bytes=limit * 2**20),
        cost_estimate=pl.CostEstimate(flops=flops, bytes_accessed=0, transcendentals=0),
        name=name,
    )(*args)


def chunk_spans(columns, shares=(0.32, 0.685)):
    ends = [0] + [64 * round(columns * share / 64) for share in shares] + [columns]
    return [(a, b - a) for a, b in zip(ends, ends[1:])]


def even(size, most):
    step = -(-size // (16 * -(-size // most))) * 16
    return [(at, min(step, size - at)) for at in range(0, size, step)]


def tie(*values):
    return lax.optimization_barrier(values)


def on_device(mesh, hidden, norm_gain, head_weight, token_ids, seq_lengths):
    rows, width = hidden.shape
    columns = head_weight.shape[1]
    plan = Plan(mesh, rows, columns)
    W, part, blocks = plan.W, plan.part, plan.blocks
    depth = width * W
    shape = jax.ShapeDtypeStruct
    move = lambda value, perm: lax.ppermute(value, AXES, perm)

    sent = call(
        functools.partial(send_kernel, plan),
        [shape((part + EXTRA, width), jnp.bfloat16)] * W,
        [pltpu.with_memory_space_constraint(x, pltpu.HBM) for x in (hidden, norm_gain, token_ids)],
        0,
        scratch=[
            pltpu.VMEM((width,), jnp.float32),
            pltpu.VMEM(token_ids.shape, jnp.int32),
            pltpu.SemaphoreType.DMA((2 + W,)),
        ],
        name="send",
        far=3,
    )
    pieces = {k: move(sent[k], plan.width_xor(k)) for k in sorted(range(1, W), key=lambda k: (k != 1, -k))}
    pieces = [sent[0]] + [pieces[k] for k in range(1, W)]
    normed, all_ids = call(
        functools.partial(norm_kernel, plan, depth),
        [shape((depth, part), jnp.bfloat16), shape((W * blocks, part), jnp.int32)],
        pieces,
        0,
        name="norm",
    )

    spans = chunk_spans(columns)
    weight = head_weight.T
    bits = [1 << i for i in range(W.bit_length() - 1)]
    near = move(weight, plan.width_xor(1))

    def far_chunk(c, after):
        a, n = spans[c]
        held = {0: tie(weight[a : a + n], *after)[0]}
        for bit in reversed(bits[1:]):
            for k in list(held):
                held[k | bit] = move(held[k], plan.width_xor(bit))
        return held

    def near_chunk(c, held):
        start, size = spans[c]
        for at, count in even(size, NEAR):
            refs = {0: (weight, start + at), 1: (near, start + at)}
            for k in held:
                if k:
                    refs[k] = (held[k], at)
                    refs[k | 1] = (move(held[k][at : at + count], plan.width_xor(1)), 0)
            chunks.append([refs[k][0] for k in range(W)])
            firsts.append([refs[k][1] for k in range(W)])
            parts.append((start + at, count))

    states, groups, chunks, firsts, parts, done = {}, {}, [], [], [], {}

    def stage(wanted, last=False):
        jobs = {key: [c for c in mine if c not in done.get(key, [])] for key, mine in wanted.items()}
        done.update(wanted)
        keys = list(jobs)
        used = sorted({c for mine in jobs.values() for c in mine})
        have = [key in states for key in keys]
        sizes, bases = [parts[c][1] for c in used], [parts[c][0] for c in used]
        args = [seq_lengths, all_ids] + [part for key in keys if jobs[key] for part in groups[key]]
        halves = [len(groups[key]) if jobs[key] else 0 for key in keys]
        held = [chunks[c][k] for c in used for k in range(W)]
        offsets = [firsts[c] for c in used]
        unique = [held[i] for i in range(len(held)) if all(held[i] is not held[j] for j in range(i))]
        where = [next(j for j in range(len(unique)) if unique[j] is one) for one in held]
        args += unique
        args += [states[key] for key in keys if key in states]
        if last:
            out = [shape((4, plan.V, part), jnp.float32)]
        else:
            out = [shape((4, 8, part), jnp.float32)] * len(keys)
        work = sum(parts[c][1] for mine in jobs.values() for c in mine)
        got = call(
            functools.partial(
                main_kernel, plan, [[used.index(c) for c in jobs[key]] for key in keys], sizes, bases, have, last, keys,
                halves, where,
                offsets
            ),
            out,
            args,
            1,
            scratch=[pltpu.VMEM((TILE, part), jnp.float32)] * 2,
            flops=0,
            name="logits",
        )
        if last:
            return got[0]
        states.update(zip(keys, got))

    groups[0, 0] = [normed]
    ring, far = normed, {}
    fast = plan.X == 2 and plan.Z == 4
    for dz in range(plan.Z):
        end = dz == plan.Z - 1
        onward, arrived, tied = [], {}, {}
        if not end:
            onward = [move(ring, plan.z_ring())]
        if end and plan.X == 2:
            half = depth // 2
            arrived[dz, 1] = [
                move(ring[:half], plan.x_ring()),
                move(groups[dz - 1, 1][0][half:], plan.z_ring()),
            ]
        else:
            passed = ring
            for dx in range(1, plan.X):
                passed = move(passed, plan.x_ring())
                arrived[dz, dx] = [passed]
        if far:
            near_chunk(dz - 1, far)
        whole = len(chunks)
        if dz == 0:
            tied["near"] = near
        if dz < len(spans):
            tied["far"] = far_chunk(dz, pieces[-1:])
        if fast and dz:
            stage({key: list(range(whole)) for key in groups})
            tied["states"] = states
        onward, arrived, tied = lax.optimization_barrier((onward, arrived, tied))
        states = tied.get("states", states)
        far = tied.get("far", {})
        near = tied.get("near", near)
        groups.update(arrived)
        if not end:
            ring = onward[0]
            groups[dz + 1, 0] = onward
    stats = stage({key: list(range(len(chunks))) for key in groups}, last=True)

    levels = [1 << i for i in range(plan.V.bit_length() - 1)]
    if W == 4 and plan.V == 8:
        parts = [stats] + [move(stats, plan.vocab_xor(k)) for k in (3, 2, 1)]
        mine, other = call(
            functools.partial(split_kernel, plan, 4),
            [shape((4, plan.V // 2, part), jnp.float32)] * 2,
            parts,
            0,
            name="split",
        )
        arrived = [
            move(other, plan.perm(lambda v, w: (v ^ 4, w ^ 2))),
            move(mine, plan.vocab_xor(4)),
            move(other, plan.width_xor(2)),
        ]
        keep, passed = call(
            functools.partial(pair_kernel, plan),
            [shape((4 * blocks, part), jnp.float32)] * 2,
            (*arrived, mine),
            0,
            name="pair",
        )
        closed, order = [keep, move(passed, plan.width_xor(1))], (0, 2, 1, 3)
    else:
        rounds = [levels[i : i + 2] for i in range(0, len(levels), 2)]
        for i, level in enumerate(rounds):
            others = [level[0]] if len(level) == 1 else [level[0], level[1], level[0] | level[1]]
            parts = [stats] + [move(stats, plan.vocab_xor(k)) for k in others]
            if i + 1 < len(rounds):
                stats = call(
                    functools.partial(merge_kernel, len(parts)), shape(stats.shape, jnp.float32), parts, 0, name="merge"
                )
        closed = call(
            functools.partial(close_kernel, plan, len(parts)),
            [shape((2 * blocks, part), jnp.float32)] * W,
            parts,
            0,
            scratch=[pltpu.VMEM((2, plan.V, part), jnp.float32)],
            name="close",
        )
        closed = [closed[0]] + [move(closed[k], plan.width_xor(k)) for k in range(1, W)]
        order = tuple(range(W))
    return tuple(
        call(
            functools.partial(place_kernel, plan, len(closed), order),
            [shape(token_ids.shape, jnp.float32)] * 2,
            (seq_lengths, *closed),
            1,
            name="place",
        )
    )


def solution(mesh):
    in_specs = (P("vocab", "width"), P("width"), P("width", "vocab"), P("width"), P())
    out_specs = (P("width"), P("width"))
    return jax.shard_map(
        functools.partial(on_device, mesh), mesh=mesh, in_specs=in_specs, out_specs=out_specs, check_vma=False
    )
```
